128 devices in a mesh: rack: 8 (over x_lo, y), dp: 16 (over z, x_hi, core).
Axes of the slice: x: 4 (x_hi: 2, x_lo: 2; x = x_hi * 2 + x_lo), y: 4, z: 4, core: 2. Of those that a mesh axis runs over, the one named last changes fastest.
Arguments:
- grad_part: bfloat16 [8, 16, 512, 8192], P('rack', 'dp'), may hold values from -6 to 6
- weight: float32 [8, 512, 8192], P('rack', 'dp'), may hold values from -6 to 6
- moment_one: float32 [8, 512, 8192], P('rack', 'dp'), may hold values from -4 to 4
- moment_two: float32 [8, 512, 8192], P('rack', 'dp'), may hold values from 0.01 to 1
- code: float32 [4, 8], replicated, may hold values from 0.125 to 8, as said below
- owner: int32 [8, 16], P('rack'), may hold values from 0 to 15, each once within a row
- holder: int32 [16, 8], P('dp'), may hold values from 0 to 7, each once within a row
Outputs:
- weight_new: float32 [8, 512, 8192], P('rack', 'dp')
- moment_one_new: float32 [8, 512, 8192], P('rack', 'dp')
- moment_two_new: float32 [8, 512, 8192], P('rack', 'dp')
- parity: float32 [4, 3, 512, 8192], P(None, None, 'dp', 'rack')
The draws below stay inside these ranges and needn't reach their ends.
Inputs may be any that keep to these rules, and one draw needn't show every extreme that they name: code[j, r] = t_r ** j for distinct positive nodes t_r.
All inputs are finite; a program needn't handle non-finite values.
Results may differ from the reference program's by a relative error of at most 0.0003.
Values sent between devices are 32-bit elements; how exact they have to be, the bound alone decides.
No kernel may reach another device: no remote copies, remote signals or barrier semaphores. Data moves between devices by JAX's collectives and lax.ppermute only.
A program may use at most 128 MiB of HBM per device.

```python
import math
import jax
import jax.numpy as jnp
from jax import lax

D = 8192
ROWS = 512
CODE_ROWS = 4
STATES = 3
N_RACK = 8
N_DP = 16


def draw_code(key, part):
    key = jax.random.fold_in(key, 7)
    nodes = jax.random.uniform(key, (N_RACK,), jnp.float32, 0.5, 1.5)
    powers = jnp.arange(CODE_ROWS, dtype=jnp.float32)[:, None]
    return (nodes[None, :] ** powers).astype(jnp.float32)


def raised(array, rng, source, target, parts, factor):
    owner, partner = [(jnp.arange(array.shape[position]) // (array.shape[position] // parts)).reshape([-1 if axis == position else 1 for axis in range(array.ndim)]) for position in (source, target)]
    chosen = jax.random.permutation(rng, parts)[partner]
    strong = (owner == chosen) | (owner == (partner + parts // 2) % parts)
    return jnp.where(strong, factor * array, array)


def block_scale(key, extent, cuts, least, largest):
    def one(dim, shards_of):
        heights = jax.random.uniform(jax.random.fold_in(jax.random.fold_in(key, 6), dim), (shards_of,), jnp.float32, least / len(cuts), largest / len(cuts))
        return jnp.repeat(jnp.exp(heights), extent[dim] // shards_of).reshape((-1,) + (1,) * (len(extent) - dim - 1))

    gain = one(*cuts[0])
    for cut in cuts[1:]:
        gain = gain * one(*cut)
    return gain


def scatter_about(key, extent, width, limit, shards=(), held_as=jnp.bfloat16):
    result = jax.random.normal(key, extent, jnp.float32) * width
    if len(shards) > 0:
        result = block_scale(key, extent, shards, -0.22, 0.18) * result
    return jnp.clip(result, min=-limit, max=limit).astype(held_as)


def gaussian_with(own_key, dims, spread, reach, split, heavy, kind=jnp.bfloat16):
    drawn = spread * jax.random.normal(own_key, dims, jnp.float32)
    if split:
        drawn = drawn * block_scale(own_key, dims, split, -0.22, 0.18)
    return jnp.clip(raised(drawn, jax.random.fold_in(own_key, 3), *heavy), -reach, reach).astype(kind)


def setup_inputs(seed: int = 0) -> dict:
    keys = jax.random.split(jax.random.key(seed), 8)
    grad_part = gaussian_with(keys[0], (N_RACK, N_DP, ROWS, D), 1.0, 6.0, ((0, 8), (1, 16)), (1, 2, 16, 2.0))
    weight = scatter_about(keys[1], (N_RACK, ROWS, D), 1.0, 6.0, ((0, 8), (1, 16)), jnp.float32)
    moment_one = scatter_about(keys[2], (N_RACK, ROWS, D), 0.3, 4.0, ((0, 8), (1, 16)), jnp.float32)
    moment_two = jnp.clip(jnp.exp(math.log(1.0) - 4.6051702 * jax.random.uniform(keys[3], (N_RACK, ROWS, D), jnp.float32) ** block_scale(keys[3], (N_RACK, ROWS, D), ((0, 8), (1, 16)), -0.2, 0.2)), 0.01, 1.0)
    code = draw_code(jax.random.fold_in(keys[7], 71), 0)
    owner = jax.vmap(lambda own: jax.random.permutation(own, N_DP))(jax.random.split(keys[5], N_RACK)).reshape((N_RACK, N_DP)).astype(jnp.int32)
    holder = jax.vmap(lambda own: jax.random.permutation(own, N_RACK))(jax.random.split(keys[6], N_DP)).reshape((N_DP, N_RACK)).astype(jnp.int32)
    return dict(grad_part=grad_part, weight=weight, moment_one=moment_one, moment_two=moment_two, code=code, owner=owner, holder=holder)


def reference(grad_part, weight, moment_one, moment_two, code, owner, holder):
    grad_sum = lax.map(lambda piece: lax.optimization_barrier(jnp.sum(piece.astype(jnp.float32), axis=0)), grad_part)
    blocks = grad_sum.reshape(N_RACK, N_DP, ROWS // N_DP, D)
    inverse_owner = jnp.argsort(owner, axis=1).astype(jnp.int32)
    owned = jnp.take_along_axis(blocks, inverse_owner[:, :, None, None], axis=1).reshape(N_RACK, ROWS, D)
    moment_one_new = 0.9 * moment_one + 0.1 * owned
    moment_two_new = 0.95 * moment_two + 0.05 * owned * owned
    step_size = moment_one_new / (1.0 - 0.9 ** 10) / (jnp.sqrt(moment_two_new / (1.0 - 0.95 ** 10)) + 1e-08)
    weight_new = weight - 0.01 * (step_size + 0.1 * weight)
    states = jnp.stack([weight_new, moment_one_new, moment_two_new])
    coded = jnp.einsum('jr,krnd->jknd', code, states, precision=lax.Precision.HIGHEST)
    coded = coded.reshape(CODE_ROWS, STATES, N_DP, ROWS // N_DP, N_RACK, D // N_RACK)
    inverse_holder = jnp.argsort(holder, axis=1).astype(jnp.int32)
    placed = jnp.take_along_axis(coded, inverse_holder[None, None, :, None, :, None], axis=4)
    parity = placed.reshape(CODE_ROWS, STATES, ROWS, D)
    return (weight_new, moment_one_new, moment_two_new, parity)
```

```python
import functools

import jax
import jax.numpy as jnp
from jax import lax
from jax.experimental import pallas as pl
from jax.experimental.pallas import tpu as pltpu
from jax.sharding import PartitionSpec as P

AXES = ("rack", "dp")
F32 = jnp.float32
MIB = 1 << 20


def links(move):
    pairs = []
    for rack in range(8):
        for data in range(16):
            x, y, z, core = (data // 2 % 2) * 2 + rack // 4, rack % 4, data // 4, data % 2
            nx, ny, nz, ncore = move(x, y, z, core)
            nx, ny, nz = nx % 4, ny % 4, nz % 4
            pairs.append((rack * 16 + data, ((nx % 2) * 4 + ny) * 16 + nz * 4 + (nx // 2) * 2 + ncore))
    return pairs


TO_CORE = links(lambda x, y, z, core: (x, y, z, 1 - core))
UP_Z = links(lambda x, y, z, core: (x, y, z + 1, core))
DOWN_Z = links(lambda x, y, z, core: (x, y, z - 1, core))
ACROSS = links(lambda x, y, z, core: (x ^ 2, y, z, core))
BESIDE = links(lambda x, y, z, core: (x ^ 1, y, z, core))
CORNER = links(lambda x, y, z, core: (3 - x, y, z, core))
ALONG_Y = [None] + [links(lambda x, y, z, core, step=step: (x, y + step, z, core)) for step in (1, 2, 3)]


def send(array, pairs):
    return lax.ppermute(array, AXES, pairs)


def call(body, scalars, grid, ins, outs, after=(), aliases=None, flops=0, moved=0, limit=32):
    n_in, n_after = len(ins), len(after)

    def kernel(*refs):
        marks = refs[: len(scalars)]
        rest = refs[len(scalars) :]
        body(marks, rest[:n_in], rest[n_in + n_after :])

    return pl.pallas_call(
        kernel,
        out_shape=[jax.ShapeDtypeStruct(shape, F32) for shape, _, _ in outs],
        grid_spec=pltpu.PrefetchScalarGridSpec(
            num_scalar_prefetch=len(scalars),
            grid=grid,
            in_specs=[
                pl.BlockSpec(memory_space=pl.ANY) if block is None else pl.BlockSpec(block, where)
                for _, block, where in ins
            ]
            + [pl.BlockSpec(memory_space=pl.ANY)] * n_after,
            out_specs=[pl.BlockSpec(block, where) for _, block, where in outs],
        ),
        input_output_aliases=aliases or {},
        compiler_params=pltpu.CompilerParams(vmem_limit_bytes=limit * MIB),
        cost_estimate=pl.CostEstimate(flops=flops, bytes_accessed=moved, transcendentals=0),
    )(*scalars, *[array for array, _, _ in ins], *after)


SEND, KEEP, PLACE, RANK = 0, 8, 16, 24
FAR, UP, DOWN, HERE = 0, 2, 4, 6


def index_vector(owner, holder):
    data, rack = lax.axis_index("dp"), lax.axis_index("rack")
    z, half, core = data // 4, data // 2 % 2, data % 2
    side, y = rack // 4, rack % 4
    k = jnp.arange(32, dtype=jnp.int32)
    kind, low = k // 8, k % 8
    far = low // 2
    relative = jnp.where(far == 0, 2, jnp.where(far == 1, 1, jnp.where(far == 2, 3, 0)))
    whose = jnp.where(kind == 0, 1 - core, core)
    target = (z + relative) % 4 * 4 + (half + low % 2) % 2 * 2 + whose
    rank = (side + low // 4) % 2 * 4 + (y + low % 4) % 4
    source = (side + low // 4) % 2 * 4 + (y - low % 4 + 4) % 4
    blocks = jnp.arange(16, dtype=jnp.int32)
    in_owner = jnp.sum(jnp.where(owner[None, :] == target[:, None], blocks[None, :], 0), axis=1)
    columns = jnp.arange(8, dtype=jnp.int32)
    in_holder = jnp.sum(jnp.where(holder[None, :] == rank[:, None], columns[None, :], 0), axis=1)
    return jnp.where(kind < 2, in_owner, jnp.where(kind == 2, in_holder, source))


def other_places(holder):
    rack = lax.axis_index("rack")
    side, y = rack // 4, rack % 4
    rank = (1 - side) * 4 + (y + jnp.arange(4, dtype=jnp.int32)) % 4
    columns = jnp.arange(8, dtype=jnp.int32)
    return jnp.sum(jnp.where(holder[None, :] == rank[:, None], columns[None, :], 0), axis=1)


def widen(marks, blocks, first, count, after=()):
    def body(marks, ins, outs):
        outs[0][...] = ins[0][...].astype(F32)

    return call(
        body,
        [marks],
        (count, 2),
        [(blocks, (1, 16, 8192), lambda i, c, m: (m[SEND + first + i], c, 0))],
        [((count, 32, 8192), (1, 16, 8192), lambda i, c, m: (i, c, 0))],
        after,
        moved=count * 3 * MIB // 2,
    )[0]


def pair_far(marks, blocks, given):
    def body(marks, ins, outs):
        total = ins[0][0].astype(F32) + ins[1][0]
        outs[0][0, 0] = total[:, :4096]
        outs[1][0, 0] = total[:, 4096:]

    half = ((2, 2, 16, 4096), (1, 1, 16, 4096), lambda i, c, m: (i, c, 0, 0))
    return call(
        body,
        [marks],
        (2, 2),
        [
            (blocks, (1, 16, 8192), lambda i, c, m: (m[KEEP + FAR + i], c, 0)),
            (given, (1, 16, 8192), lambda i, c, m: (i, c, 0)),
        ],
        [half, half],
        moved=5 * MIB,
    )


def pair_near(marks, blocks, given, after=()):
    def body(marks, ins, outs):
        outs[0][0, 0] = ins[0][0].astype(F32) + ins[1][0]
        outs[1][0, 0] = ins[2][0].astype(F32) + ins[3][0]

    half = ((2, 2, 16, 4096), (1, 1, 16, 4096), lambda i, c, m: (i, c, 0, 0))
    return call(
        body,
        [marks],
        (2, 2),
        [
            (blocks, (1, 16, 4096), lambda i, c, m: (m[KEEP + UP + i], c, 1)),
            (given, (1, 16, 4096), lambda i, c, m: (i, c, 1)),
            (blocks, (1, 16, 4096), lambda i, c, m: (m[KEEP + DOWN + i], c, 0)),
            (given, (1, 16, 4096), lambda i, c, m: (2 + i, c, 0)),
        ],
        [half, half],
        after,
        moved=5 * MIB,
    )


def onward(marks, blocks, given, from_below, from_above, c, after=()):
    def body(marks, ins, outs):
        outs[0][0] = ins[0][0].astype(F32) + ins[1][0] + ins[2][0, 0]
        outs[1][0] = ins[3][0].astype(F32) + ins[4][0] + ins[5][0, 0]

    half = ((2, 16, 4096), (1, 16, 4096), lambda i, m: (i, 0, 0))
    return call(
        body,
        [marks],
        (2,),
        [
            (blocks, (1, 16, 4096), lambda i, m: (m[KEEP + UP + i], c, 0)),
            (given, (1, 16, 4096), lambda i, m: (i, c, 0)),
            (from_below, (1, 1, 16, 4096), lambda i, m: (i, c, 0, 0)),
            (blocks, (1, 16, 4096), lambda i, m: (m[KEEP + DOWN + i], c, 1)),
            (given, (1, 16, 4096), lambda i, m: (2 + i, c, 1)),
            (from_above, (1, 1, 16, 4096), lambda i, m: (i, c, 0, 0)),
        ],
        [half, half],
        after,
        moved=4 * MIB,
    )


def gathered_z(marks, places, blocks, given, fwd_below, near_above, near_below, fwd_above, c):
    def body(marks, ins, outs):
        index, other = marks
        for j in range(2):
            mine = ins[j][0].astype(F32) + ins[2][j]
            outs[j][:, :4096] = mine[:, :4096] + ins[3][j] + ins[4][j, 0]
            outs[j][:, 4096:] = mine[:, 4096:] + ins[5][j, 0] + ins[6][j]
        for s in range(4):
            at = pl.multiple_of(index[PLACE + 4 + s] * 1024, 1024)
            outs[2][s] = outs[0][:, pl.ds(at, 1024)]
            at = pl.multiple_of(other[s] * 1024, 1024)
            outs[3][s] = outs[1][:, pl.ds(at, 1024)]

    rows = ((16, 8192), (16, 8192), lambda i, m, o: (0, 0))
    parts = ((4, 16, 1024), (4, 16, 1024), lambda i, m, o: (0, 0, 0))
    return call(
        body,
        [marks, places],
        (1,),
        [
            (blocks, (1, 16, 8192), lambda i, m, o: (m[KEEP + HERE], c, 0)),
            (blocks, (1, 16, 8192), lambda i, m, o: (m[KEEP + HERE + 1], c, 0)),
            (given, (2, 16, 8192), lambda i, m, o: (0, c, 0)),
            (fwd_below, (2, 16, 4096), lambda i, m, o: (0, 0, 0)),
            (near_above, (2, 1, 16, 4096), lambda i, m, o: (0, c, 0, 0)),
            (near_below, (2, 1, 16, 4096), lambda i, m, o: (0, c, 0, 0)),
            (fwd_above, (2, 16, 4096), lambda i, m, o: (0, 0, 0)),
        ],
        [rows, rows, parts, parts],
        moved=5 * MIB,
    )


def for_holders(marks, own, across, beside, corner):
    def body(marks, ins, outs):
        index = marks[0]
        for s in range(4):
            at = pl.multiple_of(index[PLACE + s] * 1024, 1024)
            outs[s][0] = ins[0][:, pl.ds(at, 1024)] + ins[1][:, pl.ds(at, 1024)]
            outs[s][1] = ins[2][s] + ins[3][s]

    rows = ((16, 8192), lambda i, m: (0, 0))
    parts = ((4, 16, 1024), lambda i, m: (0, 0, 0))
    return call(
        body,
        [marks],
        (1,),
        [(own, *rows), (across, *rows), (beside, *parts), (corner, *parts)],
        [((2, 16, 1024), (2, 16, 1024), lambda i, m: (0, 0, 0))] * 4,
        moved=2 * MIB,
    )


def old_beside(marks, weight, first, second, after=()):
    def body(marks, ins, outs):
        for k in range(3):
            outs[0][0, k] = ins[k][0]

    spec = ((1, 32, 1024), lambda s, m: (0, 0, m[PLACE + 4 + s]))
    return call(
        body,
        [marks],
        (4,),
        [(weight, *spec), (first, *spec), (second, *spec)],
        [((4, 3, 32, 1024), (1, 3, 32, 1024), lambda s, m: (s, 0, 0, 0))],
        after,
        moved=3 * MIB,
    )[0]


def old_for_holders(marks, weight, first, second, beside, after=()):
    def body(marks, ins, outs):
        s = pl.program_id(0)
        for at in range(4):

            @pl.when(s == at)
            def _():
                for k in range(3):
                    outs[at][0, k] = ins[k][0]
                    outs[at][1, k] = ins[3][0, k]

    spec = ((1, 32, 1024), lambda s, m: (0, 0, m[PLACE + s]))
    return call(
        body,
        [marks],
        (4,),
        [
            (weight, *spec),
            (first, *spec),
            (second, *spec),
            (beside, (1, 3, 32, 1024), lambda s, m: (s, 0, 0, 0)),
        ],
        [((2, 3, 32, 1024), (2, 3, 32, 1024), lambda s, m: (0, 0, 0, 0))] * 4,
        after,
        moved=6 * MIB,
    )


def advance(weight, first, second, grad):
    first_new = 0.9 * first + 0.1 * grad
    second_new = 0.95 * second + 0.05 * grad * grad
    step = first_new / (1.0 - 0.9**10) / (jnp.sqrt(second_new / (1.0 - 0.95**10)) + 1e-08)
    return weight - 0.01 * (step + 0.1 * weight), first_new, second_new


def update(weight, first, second, own, across, after=()):
    def body(marks, ins, outs):
        c = pl.program_id(0)
        for at in range(2):

            @pl.when(c == at)
            def _():
                grad = ins[3 + at][...] + ins[5 + at][...]
                new = advance(ins[0][0], ins[1][0], ins[2][0], grad)
                for k in range(3):
                    outs[k][0] = new[k]

    spec = ((1, 16, 2048), lambda c, i: (0, c, i))
    chunk = [
        ((16, 2048), lambda c, i: (0, jnp.where(c == 0, i, 3))),
        ((16, 2048), lambda c, i: (0, jnp.where(c == 1, i, 0))),
    ]
    return call(
        body,
        [],
        (2, 4),
        [(weight, *spec), (first, *spec), (second, *spec)]
        + [(own[at], *chunk[at]) for at in range(2)]
        + [(across[at], *chunk[at]) for at in range(2)],
        [((1, 32, 8192), *spec)] * 3,
        after,
        moved=8 * MIB,
    )


def encode(marks, code, old, grads, c, into=None):
    def body(marks, ins, outs):
        index, weights = marks
        for lane in range(0, 1024, 256):
            columns = pl.ds(lane, 256)
            for row in range(0, 16, 8):
                rows = pl.ds(row, 8)
                sums = [[None] * 3 for _ in range(4)]
                for s in range(4):
                    for a in range(2):
                        states = advance(
                            *(ins[s][a, k, rows, columns] for k in range(3)), ins[4 + s][a, rows, columns]
                        )
                        rank = index[RANK + a * 4 + s]
                        for j in range(4):
                            scale = weights[j, rank]
                            for k in range(3):
                                term = scale * states[k]
                                sums[j][k] = term if sums[j][k] is None else sums[j][k] + term
                for j in range(4):
                    for k in range(3):
                        outs[0][j, k, rows, columns] = sums[j][k]

    return call(
        body,
        [marks, code],
        (1,),
        [(array, (2, 3, 16, 1024), lambda i, m, w: (0, 0, c, 0)) for array in old]
        + [(array, (2, 16, 1024), lambda i, m, w: (0, 0, 0)) for array in grads]
        + ([] if into is None else [(into, None, None)]),
        [((4, 3, 32, 1024), (4, 3, 16, 1024), lambda i, m, w: (0, 0, c, 0))],
        aliases=None if into is None else {10: 0},
        moved=3 * MIB,
    )[0]


def local(grad_part, weight, moment_one, moment_two, code, owner, holder):
    marks = index_vector(owner[0], holder[0])
    blocks = grad_part.reshape(16, 32, 8192)

    far = send(widen(marks, blocks, FAR, 2), TO_CORE)
    near = send(widen(marks, blocks, UP, 4), TO_CORE)
    here = send(widen(marks, blocks, HERE, 2), TO_CORE)

    go_up, go_down = pair_far(marks, blocks, far)
    far_below, far_above = send(go_up, UP_Z), send(go_down, DOWN_Z)

    beside = send(old_beside(marks, weight, moment_one, moment_two, (go_up,)), BESIDE)

    go_up, go_down = pair_near(marks, blocks, near, (go_up,))
    near_below, near_above = send(go_up, UP_Z), send(go_down, DOWN_Z)

    places = other_places(send(holder[0], ACROSS))

    fwd = []
    for c in range(2):
        go_up, go_down = onward(marks, blocks, near, far_below, far_above, c)
        fwd.append((send(go_up, UP_Z), send(go_down, DOWN_Z)))

    old = old_for_holders(marks, weight, moment_one, moment_two, beside)
    old = [old[0]] + [send(old[s], ALONG_Y[s]) for s in (1, 2, 3)]

    own, across, grads = [], [], []
    for c in range(2):
        mine, theirs, to_beside, to_corner = gathered_z(
            marks, places, blocks, here, fwd[c][0], near_above, near_below, fwd[c][1], c
        )
        own.append(mine)
        across.append(send(theirs, ACROSS))
        from_beside, from_corner = send(to_beside, BESIDE), send(to_corner, CORNER)
        parts = for_holders(marks, mine, across[c], from_beside, from_corner)
        grads.append([parts[0]] + [send(parts[s], ALONG_Y[s]) for s in (1, 2, 3)])

    new = update(weight, moment_one, moment_two, own, across)
    parity = encode(marks, code, old, grads[0], 0)
    parity = encode(marks, code, old, grads[1], 1, parity)
    return (*new, parity)


def solution(mesh):
    in_specs = (
        P("rack", "dp", None, None),
        P("rack", "dp", None),
        P("rack", "dp", None),
        P("rack", "dp", None),
        P(),
        P("rack", None),
        P("dp", None),
    )
    out_specs = (
        P("rack", "dp", None),
        P("rack", "dp", None),
        P("rack", "dp", None),
        P(None, None, "dp", "rack"),
    )
    return jax.shard_map(local, mesh=mesh, in_specs=in_specs, out_specs=out_specs, check_vma=False)
```

```python
import jax
import jax.numpy as jnp
from jax import lax
from jax.experimental import pallas as pl
from jax.experimental.pallas import tpu as pltpu
from jax.sharding import PartitionSpec as P

AXES = ("rack", "dp")
F32, BF16 = jnp.float32, jnp.bfloat16
MIB = 1 << 20
VMEM = pl.BlockSpec(memory_space=pltpu.VMEM)
SMEM = pl.BlockSpec(memory_space=pltpu.SMEM)
HBM = pl.BlockSpec(memory_space=pltpu.HBM)


def links(move):
    pairs = []
    for rack in range(8):
        for data in range(16):
            x, y, z, core = (data // 2 % 2) * 2 + rack // 4, rack % 4, data // 4, data % 2
            nx, ny, nz, ncore = move(x, y, z, core)
            nx, ny, nz = nx % 4, ny % 4, nz % 4
            pairs.append((rack * 16 + data, ((nx % 2) * 4 + ny) * 16 + nz * 4 + (nx // 2) * 2 + ncore))
    return pairs


TO_CORE = links(lambda x, y, z, core: (x, y, z, 1 - core))
UP_Z = links(lambda x, y, z, core: (x, y, z + 1, core))
DOWN_Z = links(lambda x, y, z, core: (x, y, z - 1, core))
ACROSS = links(lambda x, y, z, core: (x ^ 2, y, z, core))
BESIDE = links(lambda x, y, z, core: (x ^ 1, y, z, core))
CORNER = links(lambda x, y, z, core: (3 - x, y, z, core))
ALONG_Y = [None] + [links(lambda x, y, z, core, step=step: (x, y + step, z, core)) for step in (1, 2, 3)]

RELATIVE_Z = (2, 1, 3, 0)
FAR, UP, DOWN, HERE = 0, 2, 4, 6


def send(array, pairs):
    return lax.ppermute(array, AXES, pairs)


def call(name, body, ins, outs, scratch=(), aliases=None, limit=16):
    return pl.pallas_call(
        body,
        out_shape=[jax.ShapeDtypeStruct(shape, kind) for shape, kind, _ in outs],
        in_specs=[spec for _, spec in ins],
        out_specs=[spec for _, _, spec in outs],
        scratch_shapes=list(scratch),
        input_output_aliases=aliases or {},
        compiler_params=pltpu.CompilerParams(vmem_limit_bytes=limit * MIB),
        name=name,
    )(*[array for array, _ in ins])


def position():
    data, rack = lax.axis_index("dp"), lax.axis_index("rack")
    return lax.div(data, 4), lax.rem(lax.div(data, 2), 2), lax.rem(data, 2), lax.div(rack, 4), lax.rem(rack, 4)


def found(row, count, value):
    at = jnp.int32(0)
    for i in range(count):
        at = jnp.where(row[0, i] == value, i, at)
    return at


def block_of(owner, slot, keep):
    z, half, core, _, _ = position()
    whose = core if keep else 1 - core
    target = lax.rem(z + RELATIVE_Z[slot // 2], 4) * 4 + lax.rem(half + slot % 2, 2) * 2 + whose
    return found(owner, 16, target)


def column_of(holder, side_step, y_step):
    _, _, _, side, y = position()
    rank = lax.rem(side + side_step, 2) * 4 + lax.rem(y + y_step, 4)
    return pl.multiple_of(found(holder, 8, rank) * 1024, 1024)


def by_tiles(width, step, body):
    def one(i, carry):
        body(pl.ds(pl.multiple_of(i * step, step), step))
        return carry

    lax.fori_loop(0, width // step, one, 0)


def widen_far(blocks, owner):
    def body(blocks, owner, out, read, sems):
        copies = [
            pltpu.make_async_copy(blocks.at[block_of(owner, FAR + i, False)], read.at[i], sems.at[i]) for i in range(2)
        ]
        for copy in copies:
            copy.start()
        for i in range(2):
            copies[i].wait()

            def cast(columns):
                out[i, :, columns] = read[i, :, columns].astype(F32)

            by_tiles(8192, 1024, cast)

    return call(
        "widen_far",
        body,
        [(blocks, HBM), (owner, SMEM)],
        [((2, 32, 8192), F32, VMEM)],
        [pltpu.VMEM((2, 32, 8192), BF16), pltpu.SemaphoreType.DMA((2,))],
        limit=50,
    )[0]


def widen_rest(blocks, owner, far):
    def body(blocks, owner, far, out, own, read, sems):
        copies = [
            pltpu.make_async_copy(blocks.at[block_of(owner, UP + i, False)], read.at[i], sems.at[i]) for i in range(6)
        ] + [pltpu.make_async_copy(blocks.at[block_of(owner, i, True)], own.at[i], sems.at[6 + i]) for i in range(8)]
        for copy in copies:
            copy.start()
        for i in range(6):
            copies[i].wait()

            def cast(columns):
                out[i, :, columns] = read[i, :, columns].astype(F32)

            by_tiles(8192, 1024, cast)
        for copy in copies[6:]:
            copy.wait()

    return call(
        "widen_rest",
        body,
        [(blocks, HBM), (owner, SMEM), (far, VMEM)],
        [((6, 32, 8192), F32, VMEM), ((8, 32, 8192), BF16, VMEM)],
        [pltpu.VMEM((6, 32, 8192), BF16), pltpu.SemaphoreType.DMA((14,))],
        limit=40,
    )


def pair_far(own, far, rest):
    def body(own, far, rest, up, down, same):
        for j in range(2):

            def add(columns):
                later = pl.ds(columns.start + 4096, columns.size)
                up[j, :, columns] = own[FAR + j, :, columns].astype(F32) + far[j, :, columns]
                down[j, :, columns] = own[FAR + j, :, later].astype(F32) + far[j, :, later]

            by_tiles(4096, 512, add)

    half = ((2, 32, 4096), F32, VMEM)
    return call(
        "pair_far",
        body,
        [(own, VMEM), (far, VMEM), (rest, VMEM)],
        [half, half, (rest.shape, F32, VMEM)],
        aliases={2: 2},
    )


def onward(own, rest, below, above, c, after=()):
    def body(own, rest, below, above, *refs):
        up, down = refs[len(after) :]
        rows = pl.ds(16 * c, 16)

        def pair(slot, columns):
            return own[slot, rows, columns].astype(F32) + rest[slot - 2, rows, columns]

        for j in range(2):

            def add(columns):
                later = pl.ds(columns.start + 4096, columns.size)
                up[0, j, :, columns] = pair(UP + j, columns) + below[j, rows, columns]
                up[1, j, :, columns] = pair(UP + j, later)
                down[0, j, :, columns] = pair(DOWN + j, later) + above[j, rows, columns]
                down[1, j, :, columns] = pair(DOWN + j, columns)

            by_tiles(4096, 512, add)

    half = ((2, 2, 16, 4096), F32, VMEM)
    return call(
        f"onward_{c}",
        body,
        [(own, VMEM), (rest, VMEM), (below, VMEM), (above, VMEM)] + [(array, VMEM) for array in after],
        [half, half],
    )


def gathered_z(own, rest, holder, below, above, c, after):
    def body(own, rest, mine_held, other_held, below, above, *refs):
        mine, theirs, beside, corner = refs[len(after) :]
        rows = pl.ds(16 * c, 16)
        for j, out in enumerate((mine, theirs)):

            def add(columns):
                later = pl.ds(columns.start + 4096, columns.size)
                both = own[HERE + j, rows, columns].astype(F32) + rest[HERE - 2 + j, rows, columns]
                out[:, columns] = both + below[0, j, :, columns] + above[1, j, :, columns]
                both = own[HERE + j, rows, later].astype(F32) + rest[HERE - 2 + j, rows, later]
                out[:, later] = both + below[1, j, :, columns] + above[0, j, :, columns]

            by_tiles(4096, 512, add)
        for s in range(4):
            beside[s] = mine[:, pl.ds(column_of(mine_held, 1, s), 1024)]
            corner[s] = theirs[:, pl.ds(column_of(other_held, 1, s), 1024)]

    rows = ((16, 8192), F32, VMEM)
    parts = ((4, 16, 1024), F32, VMEM)
    return call(
        f"gathered_z_{c}",
        body,
        [(own, VMEM), (rest, VMEM), (holder[0], SMEM), (holder[1], SMEM), (below, VMEM), (above, VMEM)]
        + [(array, VMEM) for array in after],
        [rows, rows, parts, parts],
    )


def for_holders(holder, mine, across, beside, corner, after=()):
    def body(holder, mine, across, beside, corner, *refs):
        outs = refs[len(after) :]
        for s in range(4):
            columns = pl.ds(column_of(holder, 0, s), 1024)
            outs[s][0] = mine[:, columns] + across[:, columns]
            outs[s][1] = beside[s] + corner[s]

    return call(
        "for_holders",
        body,
        [(holder, SMEM)] + [(array, VMEM) for array in (mine, across, beside, corner, *after)],
        [((2, 16, 1024), F32, VMEM)] * 4,
    )


def old_parts(name, holder, states, asked, after):
    def body(holder, weight, first, second, *refs):
        outs, same, sems = refs[len(after) : -2], refs[-2], refs[-1]
        copies = []
        for out, steps in zip(outs, asked):
            for i, (a, s) in enumerate(steps):
                columns = pl.ds(column_of(holder, a, s), 1024)
                for k, old in enumerate((weight, first, second)):
                    copies.append(pltpu.make_async_copy(old.at[0, :, columns], out.at[i, k], sems.at[len(copies)]))
        for copy in copies:
            copy.start()
        for i in range(8):
            same[0, i] = holder[0, i]
        for copy in copies:
            copy.wait()

    return call(
        name,
        body,
        [(holder, SMEM)] + [(old, HBM) for old in states] + [(array, VMEM) for array in after],
        [((len(steps), 3, 32, 1024), F32, VMEM) for steps in asked] + [((1, 8), jnp.int32, SMEM)],
        [pltpu.SemaphoreType.DMA((3 * sum(len(steps) for steps in asked),))],
    )


def other_side(olds, after):
    count = len(olds)

    def body(*refs):
        out = refs[count + len(after)]
        for i in range(count):

            def copy(columns):
                for k in range(3):
                    out[i, k, :, columns] = refs[i][1, k, :, columns]

            by_tiles(1024, 256, copy)

    return call(
        "other_side",
        body,
        [(old, VMEM) for old in olds] + after,
        [((count, 3, 32, 1024), F32, VMEM)],
    )[0]


def advance(weight, first, second, grad):
    first_new = 0.9 * first + 0.1 * grad
    second_new = 0.95 * second + 0.05 * grad * grad
    step = first_new / (1.0 - 0.9**10) / (jnp.sqrt(second_new / (1.0 - 0.95**10)) + 1e-08)
    return weight - 0.01 * (step + 0.1 * weight), first_new, second_new


def update(weight, first, second, mine, across):
    def body(weight, first, second, mine_0, mine_1, across_0, across_1, *refs):
        outs, read, sems = refs[:3], refs[3], refs[4]
        reads = [pltpu.make_async_copy(old.at[0], read.at[k], sems.at[k]) for k, old in enumerate((weight, first, second))]
        for copy in reads:
            copy.start()
        for copy in reads:
            copy.wait()
        writes = []
        for c, (mine, across) in enumerate(((mine_0, across_0), (mine_1, across_1))):
            rows = pl.ds(16 * c, 16)

            def step(columns):
                new = advance(*(read[k, rows, columns] for k in range(3)), mine[:, columns] + across[:, columns])
                for k in range(3):
                    read[k, rows, columns] = new[k]

            by_tiles(8192, 512, step)
            for k in range(3):
                copy = pltpu.make_async_copy(read.at[k, rows], outs[k].at[0, rows], sems.at[3 + 3 * c + k])
                copy.start()
                writes.append(copy)
        for copy in writes:
            copy.wait()

    return call(
        "update",
        body,
        [(weight, HBM), (first, HBM), (second, HBM)] + [(array, VMEM) for array in (*mine, *across)],
        [((1, 32, 8192), F32, HBM)] * 3,
        [pltpu.VMEM((3, 32, 8192), F32), pltpu.SemaphoreType.DMA((9,))],
    )


def encode(code, old, grads, c, into=None):
    arrays, places = [], [[None] * 4, [None] * 4]
    for a in range(2):
        for s in range(4):
            array, part = old[a][s]
            known = [i for i, other in enumerate(arrays) if other is array]
            if not known:
                arrays.append(array)
            places[a][s] = (known[0] if known else len(arrays) - 1, part)

    def body(code, *refs):
        olds, ins, (out, total, sem) = refs[: len(arrays)], refs[len(arrays) :], refs[-3:]
        _, _, _, side, y = position()
        ranks = [[lax.rem(side + a, 2) * 4 + lax.rem(y + 4 - s, 4) for s in range(4)] for a in range(2)]
        scales = [[[code[j, ranks[a][s]] for s in range(4)] for a in range(2)] for j in range(4)]

        def state(s, a, k, row, columns):
            array, part = places[a][s]
            return olds[array][part, k, pl.ds(16 * c + row, 8), columns]

        for row in range(0, 16, 8):

            def one(columns):
                rows = pl.ds(row, 8)
                sums = [[None] * 3 for _ in range(4)]
                for s in range(4):
                    for a in range(2):
                        was = [state(s, a, k, row, columns) for k in range(3)]
                        states = advance(*was, ins[s][a, rows, columns])
                        for j in range(4):
                            for k in range(3):
                                term = scales[j][a][s] * states[k]
                                sums[j][k] = term if sums[j][k] is None else sums[j][k] + term
                for j in range(4):
                    for k in range(3):
                        total[j, k, rows, columns] = sums[j][k]

            by_tiles(1024, 256, one)
        copy = pltpu.make_async_copy(total, out.at[:, :, pl.ds(16 * c, 16)], sem)
        copy.start()
        copy.wait()

    return call(
        f"encode_{c}",
        body,
        [(code, SMEM)] + [(array, VMEM) for array in (*arrays, *grads)] + ([] if into is None else [(into, HBM)]),
        [((4, 3, 32, 1024), F32, HBM)],
        [pltpu.VMEM((4, 3, 16, 1024), F32), pltpu.SemaphoreType.DMA],
        aliases=None if into is None else {1 + len(arrays) + len(grads): 0},
    )[0]


def local(grad_part, weight, moment_one, moment_two, code, owner, holder):
    blocks = grad_part.reshape(16, 32, 8192)
    states = (weight, moment_one, moment_two)

    far = widen_far(blocks, owner)
    rest, own = widen_rest(blocks, owner, far)
    go_up, go_down, rest = pair_far(own, send(far, TO_CORE), rest)
    rest = send(rest, TO_CORE)
    far_below, far_above = send(go_up, UP_Z), send(go_down, DOWN_Z)

    one, three, _ = old_parts("old_odd", holder, states, [[(0, 1), (1, 1)], [(0, 3), (1, 3)]], (go_up,))
    one, three = send(one, ALONG_Y[1]), send(three, ALONG_Y[3])
    asked = [[(0, 2), (1, 2)], [(0, 0)], [(1, 0)]]
    two, zero, beside, held = old_parts("old_even", holder, states, asked, (rest,))
    beside = send(beside, BESIDE)
    two = send(two, ALONG_Y[2])
    held = send(held, ACROSS)

    go_up, go_down = onward(own, rest, far_below, far_above, 0)
    along_z = [(send(go_up, UP_Z), send(go_down, DOWN_Z))]
    odd = other_side([one, three], [(go_up, VMEM)])
    even = other_side([two], [(odd, VMEM), (beside, VMEM), (held, SMEM)])
    after = (even,)
    odd, even = send(odd, BESIDE), send(even, BESIDE)
    go_up, go_down = onward(own, rest, far_below, far_above, 1)
    along_z.append((send(go_up, UP_Z), send(go_down, DOWN_Z)))
    old = [[(zero, 0), (one, 0), (two, 0), (three, 0)], [(beside, 0), (odd, 0), (even, 0), (odd, 1)]]

    mine, across, parts = [], [], []
    for c in range(2):
        ours, theirs, to_beside, to_corner = gathered_z(own, rest, (holder, held), *along_z[c], c, after)
        after = (odd, even)
        mine.append(ours)
        across.append(send(theirs, ACROSS))
        parts.append((send(to_beside, BESIDE), send(to_corner, CORNER)))
    grads = []
    for c in range(2):
        sums = for_holders(holder, mine[c], across[c], *parts[c], () if c else (mine[1],))
        grads.append([sums[0]] + [send(sums[s], ALONG_Y[s]) for s in (1, 2, 3)])

    new = update(*states, mine, across)
    parity = encode(code, old, grads[0], 0)
    parity = encode(code, old, grads[1], 1, parity)
    return (*new, parity)


def solution(mesh):
    in_specs = (
        P("rack", "dp", None, None),
        P("rack", "dp", None),
        P("rack", "dp", None),
        P("rack", "dp", None),
        P(),
        P("rack", None),
        P("dp", None),
    )
    out_specs = (
        P("rack", "dp", None),
        P("rack", "dp", None),
        P("rack", "dp", None),
        P(None, None, "dp", "rack"),
    )
    return jax.shard_map(local, mesh=mesh, in_specs=in_specs, out_specs=out_specs, check_vma=False)
```

```python
import jax
import jax.numpy as jnp
from jax import lax
from jax.experimental import pallas as pl
from jax.experimental.pallas import tpu as pltpu
from jax.sharding import PartitionSpec as P

AXES = ("rack", "dp")
F32, BF16 = jnp.float32, jnp.bfloat16
MIB = 1 << 20
VMEM = pl.BlockSpec(memory_space=pltpu.VMEM)
SMEM = pl.BlockSpec(memory_space=pltpu.SMEM)
HBM = pl.BlockSpec(memory_space=pltpu.HBM)


def links(move):
    pairs = []
    for rack in range(8):
        for data in range(16):
            x, y, z, core = (data // 2 % 2) * 2 + rack // 4, rack % 4, data // 4, data % 2
            nx, ny, nz, ncore = move(x, y, z, core)
            nx, ny, nz = nx % 4, ny % 4, nz % 4
            pairs.append((rack * 16 + data, ((nx % 2) * 4 + ny) * 16 + nz * 4 + (nx // 2) * 2 + ncore))
    return pairs


TO_CORE = links(lambda x, y, z, core: (x, y, z, 1 - core))
UP_Z = links(lambda x, y, z, core: (x, y, z + 1, core))
DOWN_Z = links(lambda x, y, z, core: (x, y, z - 1, core))
ACROSS = links(lambda x, y, z, core: (x ^ 2, y, z, core))
BESIDE = links(lambda x, y, z, core: (x ^ 1, y, z, core))
CORNER = links(lambda x, y, z, core: (3 - x, y, z, core))
ALONG_Y = [None] + [links(lambda x, y, z, core, step=step: (x, y + step, z, core)) for step in (1, 2, 3)]

RELATIVE_Z = (2, 1, 3, 0)
FAR, UP, DOWN, HERE = 0, 2, 4, 6


def send(array, pairs):
    return lax.ppermute(array, AXES, pairs)


def call(name, body, ins, outs, scratch=(), aliases=None, limit=16):
    return pl.pallas_call(
        body,
        out_shape=[jax.ShapeDtypeStruct(shape, kind) for shape, kind, _ in outs],
        in_specs=[spec for _, spec in ins],
        out_specs=[spec for _, _, spec in outs],
        scratch_shapes=list(scratch),
        input_output_aliases=aliases or {},
        compiler_params=pltpu.CompilerParams(vmem_limit_bytes=limit * MIB),
        name=name,
    )(*[array for array, _ in ins])


def position():
    data, rack = lax.axis_index("dp"), lax.axis_index("rack")
    return lax.div(data, 4), lax.rem(lax.div(data, 2), 2), lax.rem(data, 2), lax.div(rack, 4), lax.rem(rack, 4)


def found(row, count, value):
    at = jnp.int32(0)
    for i in range(count):
        at = jnp.where(row[0, i] == value, i, at)
    return at


def block_of(owner, slot, keep):
    z, half, core, _, _ = position()
    whose = core if keep else 1 - core
    target = lax.rem(z + RELATIVE_Z[slot // 2], 4) * 4 + lax.rem(half + slot % 2, 2) * 2 + whose
    return found(owner, 16, target)


def column_of(holder, side_step, y_step):
    _, _, _, side, y = position()
    rank = lax.rem(side + side_step, 2) * 4 + lax.rem(y + y_step, 4)
    return pl.multiple_of(found(holder, 8, rank) * 1024, 1024)


def by_tiles(width, step, body):
    def one(i, carry):
        body(pl.ds(pl.multiple_of(i * step, step), step))
        return carry

    lax.fori_loop(0, width // step, one, 0)


def widen_far(blocks, owner):
    def body(blocks, owner, out, read, sems):
        copies = [
            pltpu.make_async_copy(blocks.at[block_of(owner, FAR + i, False)], read.at[i], sems.at[i]) for i in range(2)
        ]
        for copy in copies:
            copy.start()
        for i in range(2):
            copies[i].wait()

            def cast(columns):
                out[i, :, columns] = read[i, :, columns].astype(F32)

            by_tiles(8192, 1024, cast)

    return call(
        "widen_far",
        body,
        [(blocks, HBM), (owner, SMEM)],
        [((2, 32, 8192), F32, VMEM)],
        [pltpu.VMEM((2, 32, 8192), BF16), pltpu.SemaphoreType.DMA((2,))],
        limit=50,
    )[0]


def widen_rest(blocks, owner, far):
    def body(blocks, owner, far, out, own, read, sems):
        copies = [
            pltpu.make_async_copy(blocks.at[block_of(owner, UP + i, False)], read.at[i], sems.at[i]) for i in range(6)
        ] + [pltpu.make_async_copy(blocks.at[block_of(owner, i, True)], own.at[i], sems.at[6 + i]) for i in range(8)]
        for copy in copies:
            copy.start()
        for i in range(6):
            copies[i].wait()

            def cast(columns):
                out[i, :, columns] = read[i, :, columns].astype(F32)

            by_tiles(8192, 1024, cast)
        for copy in copies[6:]:
            copy.wait()

    return call(
        "widen_rest",
        body,
        [(blocks, HBM), (owner, SMEM), (far, VMEM)],
        [((6, 32, 8192), F32, VMEM), ((8, 32, 8192), BF16, VMEM)],
        [pltpu.VMEM((6, 32, 8192), BF16), pltpu.SemaphoreType.DMA((14,))],
        limit=40,
    )


def pair_far(own, far, rest):
    def body(own, far, rest, up, down, same):
        for j in range(2):

            def add(columns):
                later = pl.ds(columns.start + 4096, columns.size)
                up[j, :, columns] = own[FAR + j, :, columns].astype(F32) + far[j, :, columns]
                down[j, :, columns] = own[FAR + j, :, later].astype(F32) + far[j, :, later]

            by_tiles(4096, 512, add)

    half = ((2, 32, 4096), F32, VMEM)
    return call(
        "pair_far",
        body,
        [(own, VMEM), (far, VMEM), (rest, VMEM)],
        [half, half, (rest.shape, F32, VMEM)],
        aliases={2: 2},
    )


def onward(own, rest, below, above, c, after=()):
    def body(own, rest, below, above, *refs):
        up, down = refs[len(after) :]
        rows = pl.ds(16 * c, 16)

        def pair(slot, columns):
            return own[slot, rows, columns].astype(F32) + rest[slot - 2, rows, columns]

        for j in range(2):

            def add(columns):
                later = pl.ds(columns.start + 4096, columns.size)
                up[0, j, :, columns] = pair(UP + j, columns) + below[j, rows, columns]
                up[1, j, :, columns] = pair(UP + j, later)
                down[0, j, :, columns] = pair(DOWN + j, later) + above[j, rows, columns]
                down[1, j, :, columns] = pair(DOWN + j, columns)

            by_tiles(4096, 512, add)

    half = ((2, 2, 16, 4096), F32, VMEM)
    return call(
        f"onward_{c}",
        body,
        [(own, VMEM), (rest, VMEM), (below, VMEM), (above, VMEM)] + [(array, VMEM) for array in after],
        [half, half],
    )


def gathered_z(own, rest, holder, below, above, c, after):
    count = 2 - c

    def body(own, rest, mine_held, other_held, below, above, *refs):
        mine, near, beside, corner, theirs = refs[len(after) :]
        rows = pl.ds(16 * c, 16)
        for j, out in enumerate((mine, theirs)):

            def add(columns):
                later = pl.ds(columns.start + 4096, columns.size)
                both = own[HERE + j, rows, columns].astype(F32) + rest[HERE - 2 + j, rows, columns]
                out[:, columns] = both + below[0, j, :, columns] + above[1, j, :, columns]
                both = own[HERE + j, rows, later].astype(F32) + rest[HERE - 2 + j, rows, later]
                out[:, later] = both + below[1, j, :, columns] + above[0, j, :, columns]

            by_tiles(4096, 512, add)
        for s in range(4):
            beside[s] = mine[:, pl.ds(column_of(mine_held, 1, s), 1024)]
            near[s] = theirs[:, pl.ds(column_of(other_held, 0, s), 1024)]
            others = theirs[:, pl.ds(column_of(other_held, 1, s), 1024)]
            corner[s] = others
            if count == 2:
                near[4 + s] = others

    parts = ((4, 16, 1024), F32, VMEM)
    return call(
        f"gathered_z_{c}",
        body,
        [(own, VMEM), (rest, VMEM), (holder[0], SMEM), (holder[1], SMEM), (below, VMEM), (above, VMEM)]
        + [(array, VMEM) for array in after],
        [((16, 8192), F32, VMEM), ((4 * count, 16, 1024), F32, VMEM), parts, parts],
        [pltpu.VMEM((16, 8192), F32)],
    )


def for_holders(holder, mine, near, beside, corner, after):
    def body(holder, mine, near, beside, corner, after, *outs):
        for s in range(4):
            outs[s][0] = mine[:, pl.ds(column_of(holder, 0, s), 1024)] + near[s]
            outs[s][1] = beside[s] + corner[s]

    return call(
        "for_holders",
        body,
        [(holder, SMEM)] + [(array, VMEM) for array in (mine, near, beside, corner, after)],
        [((2, 16, 1024), F32, VMEM)] * 4,
    )


def old_parts(name, holder, states, asked, after):
    def body(holder, weight, first, second, *refs):
        outs = refs[len(after) :]
        for out, steps in zip(outs, asked):
            for i, (a, s) in enumerate(steps):
                start = column_of(holder, a, s)

                def copy(columns):
                    source = pl.ds(pl.multiple_of(start + columns.start, 128), columns.size)
                    for k, old in enumerate((weight, first, second)):
                        out[i, k, :, columns] = old[0, :, source]

                by_tiles(1024, 256, copy)

    return call(
        name,
        body,
        [(holder, SMEM)] + [(old, VMEM) for old in states] + [(array, VMEM) for array in after],
        [((len(steps), 3, 32, 1024), F32, VMEM) for steps in asked],
    )


def other_side(olds, after):
    count = len(olds)

    def body(*refs):
        out = refs[count + len(after)]
        for i in range(count):

            def copy(columns):
                for k in range(3):
                    out[i, k, :, columns] = refs[i][1, k, :, columns]

            by_tiles(1024, 256, copy)

    return call(
        "other_side",
        body,
        [(old, VMEM) for old in olds] + after,
        [((count, 3, 32, 1024), F32, VMEM)],
    )[0]


def advance(weight, first, second, grad):
    first_new = 0.9 * first + 0.1 * grad
    second_new = 0.95 * second + 0.05 * grad * grad
    step = first_new / (1.0 - 0.9**10) / (jnp.sqrt(second_new / (1.0 - 0.95**10)) + 1e-08)
    return weight - 0.01 * (step + 0.1 * weight), first_new, second_new


def update(holder, weight, first, second, mine, across):
    def body(holder, weight, first, second, mine_0, mine_1, all_0, near_1, far_1, *refs):
        outs, made, sems = refs[:3], refs[3], refs[4]
        writes = []
        for c, mine in enumerate((mine_0, mine_1)):
            rows = pl.ds(16 * c, 16)
            for i in range(8):
                columns = pl.ds(column_of(holder, i // 4, i % 4), 1024)
                more = all_0[i] if c == 0 else (near_1, far_1)[i // 4][i % 4]
                new = advance(*(old[0, rows, columns] for old in (weight, first, second)), mine[:, columns] + more)
                for k in range(3):
                    made[k, rows, columns] = new[k]
            for k in range(3):
                copy = pltpu.make_async_copy(made.at[k, rows], outs[k].at[0, rows], sems.at[3 * c + k])
                copy.start()
                writes.append(copy)
        for copy in writes:
            copy.wait()

    return call(
        "update",
        body,
        [(holder, SMEM)] + [(array, VMEM) for array in (weight, first, second, *mine, *across)],
        [((1, 32, 8192), F32, HBM)] * 3,
        [pltpu.VMEM((3, 32, 8192), F32), pltpu.SemaphoreType.DMA((6,))],
    )


def encode(code, old, grads, c, into=None):
    arrays, places = [], [[None] * 4, [None] * 4]
    for a in range(2):
        for s in range(4):
            array, part = old[a][s]
            known = [i for i, other in enumerate(arrays) if other is array]
            if not known:
                arrays.append(array)
            places[a][s] = (known[0] if known else len(arrays) - 1, part)

    def body(code, *refs):
        olds, ins, (out, total, sem) = refs[: len(arrays)], refs[len(arrays) :], (refs[-4], *refs[-2:])
        _, _, _, side, y = position()
        ranks = [[lax.rem(side + a, 2) * 4 + lax.rem(y + 4 - s, 4) for s in range(4)] for a in range(2)]
        scales = [[[code[j, ranks[a][s]] for s in range(4)] for a in range(2)] for j in range(4)]

        def state(s, a, k, row, columns):
            array, part = places[a][s]
            return olds[array][part, k, pl.ds(16 * c + row, 8), columns]

        for row in range(0, 16, 8):

            def one(columns):
                rows = pl.ds(row, 8)
                sums = [[None] * 3 for _ in range(4)]
                for s in range(4):
                    for a in range(2):
                        was = [state(s, a, k, row, columns) for k in range(3)]
                        states = advance(*was, ins[s][a, rows, columns])
                        for j in range(4):
                            for k in range(3):
                                term = scales[j][a][s] * states[k]
                                sums[j][k] = term if sums[j][k] is None else sums[j][k] + term
                for j in range(4):
                    for k in range(3):
                        total[j, k, rows, columns] = sums[j][k]

            by_tiles(1024, 256, one)
        copy = pltpu.make_async_copy(total, out.at[:, :, pl.ds(16 * c, 16)], sem)
        copy.start()
        copy.wait()
        refs[-3][...] = jnp.zeros((8, 128), F32)

    return call(
        f"encode_{c}",
        body,
        [(code, SMEM)] + [(array, VMEM) for array in (*arrays, *grads)] + ([] if into is None else [(into, HBM)]),
        [((4, 3, 32, 1024), F32, HBM), ((8, 128), F32, VMEM)],
        [pltpu.VMEM((4, 3, 16, 1024), F32), pltpu.SemaphoreType.DMA],
        aliases=None if into is None else {1 + len(arrays) + len(grads): 0},
    )


def local(grad_part, weight, moment_one, moment_two, code, owner, holder):
    blocks = grad_part.reshape(16, 32, 8192)
    states = (weight, moment_one, moment_two)

    far = widen_far(blocks, owner)
    rest, own = widen_rest(blocks, owner, far)
    go_up, go_down, rest = pair_far(own, send(far, TO_CORE), rest)
    rest = send(rest, TO_CORE)
    far_below, far_above = send(go_up, UP_Z), send(go_down, DOWN_Z)

    one, three = old_parts("old_odd", holder, states, [[(0, 1), (1, 1)], [(0, 3), (1, 3)]], (go_up,))
    one, three = send(one, ALONG_Y[1]), send(three, ALONG_Y[3])
    zero, beside = old_parts("old_here", holder, states, [[(0, 0)], [(1, 0)]], (rest,))
    beside = send(beside, BESIDE)

    held = send(holder, ACROSS)
    odd = other_side([one, three], [(beside, VMEM), (held, SMEM)])
    (two,) = old_parts("old_two", holder, states, [[(0, 2), (1, 2)]], (odd,))
    after = (two,)
    odd, two = send(odd, BESIDE), send(two, ALONG_Y[2])

    go_up, go_down = onward(own, rest, far_below, far_above, 0, after)
    along_z = [(send(go_up, UP_Z), send(go_down, DOWN_Z))]
    even = other_side([two], [(odd, VMEM), (go_up, VMEM)])
    after = (even,)
    even = send(even, BESIDE)
    go_up, go_down = onward(own, rest, far_below, far_above, 1, after)
    along_z.append((send(go_up, UP_Z), send(go_down, DOWN_Z)))
    old = [[(zero, 0), (one, 0), (two, 0), (three, 0)], [(beside, 0), (odd, 0), (even, 0), (odd, 1)]]

    mine, across, parity = [], [], None
    for c in range(2):
        ours, near, to_beside, to_corner = gathered_z(own, rest, (holder, held), *along_z[c], c, after)
        mine.append(ours)
        across.append(send(near, ACROSS))
        done = even if c == 0 else done
        sums = for_holders(holder, ours, across[c], send(to_beside, BESIDE), send(to_corner, CORNER), done)
        after = (sums[1],)
        grads = [sums[0]] + [send(sums[s], ALONG_Y[s]) for s in (1, 2, 3)]
        parity, done = encode(code, old, grads, c, parity)
    across.append(send(to_corner, ACROSS))

    new = update(holder, *states, mine, across)
    return (*new, parity)


def solution(mesh):
    in_specs = (
        P("rack", "dp", None, None),
        P("rack", "dp", None),
        P("rack", "dp", None),
        P("rack", "dp", None),
        P(),
        P("rack", None),
        P("dp", None),
    )
    out_specs = (
        P("rack", "dp", None),
        P("rack", "dp", None),
        P("rack", "dp", None),
        P(None, None, "dp", "rack"),
    )
    return jax.shard_map(local, mesh=mesh, in_specs=in_specs, out_specs=out_specs, check_vma=False)
```

```python
import jax
import jax.numpy as jnp
from jax import lax
from jax.experimental import pallas as pl
from jax.experimental.pallas import tpu as pltpu
from jax.sharding import PartitionSpec as P

AXES = ("rack", "dp")
F32, BF16 = jnp.float32, jnp.bfloat16
MIB = 1 << 20
VMEM = pl.BlockSpec(memory_space=pltpu.VMEM)
SMEM = pl.BlockSpec(memory_space=pltpu.SMEM)
HBM = pl.BlockSpec(memory_space=pltpu.HBM)


def links(move):
    pairs = []
    for rack in range(8):
        for data in range(16):
            x, y, z, core = (data // 2 % 2) * 2 + rack // 4, rack % 4, data // 4, data % 2
            nx, ny, nz, ncore = move(x, y, z, core)
            nx, ny, nz = nx % 4, ny % 4, nz % 4
            pairs.append((rack * 16 + data, ((nx % 2) * 4 + ny) * 16 + nz * 4 + (nx // 2) * 2 + ncore))
    return pairs


TO_CORE = links(lambda x, y, z, core: (x, y, z, 1 - core))
UP_Z = links(lambda x, y, z, core: (x, y, z + 1, core))
DOWN_Z = links(lambda x, y, z, core: (x, y, z - 1, core))
ACROSS = links(lambda x, y, z, core: (x ^ 2, y, z, core))
BESIDE = links(lambda x, y, z, core: (x ^ 1, y, z, core))
CORNER = links(lambda x, y, z, core: (3 - x, y, z, core))
BESIDE_FAR = links(lambda x, y, z, core: (x ^ 1, y + 2, z, core))
ALONG_Y = [None] + [links(lambda x, y, z, core, step=step: (x, y + step, z, core)) for step in (1, 2, 3)]

RELATIVE_Z = (2, 1, 3, 0)
FAR, UP, DOWN, HERE = 0, 2, 4, 6


def send(array, pairs):
    return lax.ppermute(array, AXES, pairs)


def call(name, body, ins, outs, scratch=(), aliases=None, limit=16):
    return pl.pallas_call(
        body,
        out_shape=[jax.ShapeDtypeStruct(shape, kind) for shape, kind, _ in outs],
        in_specs=[spec for _, spec in ins],
        out_specs=[spec for _, _, spec in outs],
        scratch_shapes=list(scratch),
        input_output_aliases=aliases or {},
        compiler_params=pltpu.CompilerParams(vmem_limit_bytes=limit * MIB),
        name=name,
    )(*[array for array, _ in ins])


def position():
    data, rack = lax.axis_index("dp"), lax.axis_index("rack")
    return lax.div(data, 4), lax.rem(lax.div(data, 2), 2), lax.rem(data, 2), lax.div(rack, 4), lax.rem(rack, 4)


def found(row, count, value):
    at = jnp.int32(0)
    for i in range(count):
        at = jnp.where(row[0, i] == value, i, at)
    return at


def block_of(owner, slot, keep):
    z, half, core, _, _ = position()
    whose = core if keep else 1 - core
    target = lax.rem(z + RELATIVE_Z[slot // 2], 4) * 4 + lax.rem(half + slot % 2, 2) * 2 + whose
    return found(owner, 16, target)


def column_of(holder, side_step, y_step):
    _, _, _, side, y = position()
    rank = lax.rem(side + side_step, 2) * 4 + lax.rem(y + y_step, 4)
    return pl.multiple_of(found(holder, 8, rank) * 1024, 1024)


def by_tiles(width, step, body):
    def one(i, carry):
        body(pl.ds(pl.multiple_of(i * step, step), step))
        return carry

    lax.fori_loop(0, width // step, one, 0)


def widen_far(blocks, owner):
    def body(blocks, owner, out, own, read, sems):
        copies = []
        for keep, to in ((False, read), (True, own)):
            for i in range(2):
                source = blocks.at[block_of(owner, FAR + i, keep)]
                copies.append(pltpu.make_async_copy(source, to.at[i], sems.at[len(copies)]))
                copies[-1].start()
        for i in range(2):
            copies[i].wait()

            def cast(columns):
                out[i, :, columns] = read[i, :, columns].astype(F32)

            by_tiles(8192, 1024, cast)
        for copy in copies[2:]:
            copy.wait()

    return call(
        "widen_far",
        body,
        [(blocks, HBM), (owner, SMEM)],
        [((2, 32, 8192), F32, VMEM), ((2, 32, 8192), BF16, VMEM)],
        [pltpu.VMEM((2, 32, 8192), BF16), pltpu.SemaphoreType.DMA((4,))],
        limit=48,
    )


def widen_rest(blocks, owner, after):
    def body(blocks, owner, after, out, read, sems):
        copies = []
        for i in range(6):
            source = blocks.at[block_of(owner, UP + i, False)]
            copies.append(pltpu.make_async_copy(source, read.at[i], sems.at[i]))
            copies[-1].start()
        for i in range(6):
            copies[i].wait()

            def cast(columns):
                out[i, :, columns] = read[i, :, columns].astype(F32)

            by_tiles(8192, 1024, cast)

    return call(
        "widen_rest",
        body,
        [(blocks, HBM), (owner, SMEM), (after, VMEM)],
        [((6, 32, 8192), F32, VMEM)],
        [pltpu.VMEM((6, 32, 8192), BF16), pltpu.SemaphoreType.DMA((6,))],
        limit=42,
    )[0]


def own_rest(blocks, owner, after):
    def body(blocks, owner, after, own, sems):
        copies = []
        for i in range(6):
            source = blocks.at[block_of(owner, UP + i, True)]
            copies.append(pltpu.make_async_copy(source, own.at[i], sems.at[i]))
            copies[-1].start()
        for copy in copies:
            copy.wait()

    return call(
        "own_rest",
        body,
        [(blocks, HBM), (owner, SMEM), (after, VMEM)],
        [((6, 32, 8192), BF16, VMEM)],
        [pltpu.SemaphoreType.DMA((6,))],
    )[0]


def pair_far(own, far, rest):
    def body(own, far, rest, up, down, same):
        for j in range(2):

            def add(columns):
                later = pl.ds(columns.start + 4096, columns.size)
                up[j, :, columns] = own[j, :, columns].astype(F32) + far[j, :, columns]
                down[j, :, columns] = own[j, :, later].astype(F32) + far[j, :, later]

            by_tiles(4096, 512, add)

    half = ((2, 32, 4096), F32, VMEM)
    return call(
        "pair_far",
        body,
        [(own, VMEM), (far, VMEM), (rest, VMEM)],
        [half, half, (rest.shape, F32, VMEM)],
        aliases={2: 2},
    )


def onward(own, rest, below, above, c, after=()):
    def body(own, rest, below, above, *refs):
        up, down = refs[len(after) :]
        rows = pl.ds(16 * c, 16)

        def pair(slot, columns):
            return own[slot - 2, rows, columns].astype(F32) + rest[slot - 2, rows, columns]

        for j in range(2):

            def add(columns):
                later = pl.ds(columns.start + 4096, columns.size)
                up[0, j, :, columns] = pair(UP + j, columns) + below[j, rows, columns]
                up[1, j, :, columns] = pair(UP + j, later)
                down[0, j, :, columns] = pair(DOWN + j, later) + above[j, rows, columns]
                down[1, j, :, columns] = pair(DOWN + j, columns)

            by_tiles(4096, 512, add)

    half = ((2, 2, 16, 4096), F32, VMEM)
    return call(
        f"onward_{c}",
        body,
        [(own, VMEM), (rest, VMEM), (below, VMEM), (above, VMEM)] + [(array, VMEM) for array in after],
        [half, half],
    )


def gathered_z(own, rest, holder, below, above, c, after):
    count = 2 - c

    def body(own, rest, mine_held, other_held, below, above, *refs):
        mine, near, beside, corner, theirs = refs[len(after) :]
        rows = pl.ds(16 * c, 16)
        for j, out in enumerate((mine, theirs)):

            def add(columns):
                later = pl.ds(columns.start + 4096, columns.size)
                both = own[HERE - 2 + j, rows, columns].astype(F32) + rest[HERE - 2 + j, rows, columns]
                out[:, columns] = both + below[0, j, :, columns] + above[1, j, :, columns]
                both = own[HERE - 2 + j, rows, later].astype(F32) + rest[HERE - 2 + j, rows, later]
                out[:, later] = both + below[1, j, :, columns] + above[0, j, :, columns]

            by_tiles(4096, 512, add)
        for s in range(4):
            beside[s] = mine[:, pl.ds(column_of(mine_held, 1, s), 1024)]
            near[s] = theirs[:, pl.ds(column_of(other_held, 0, s), 1024)]
            others = theirs[:, pl.ds(column_of(other_held, 1, s), 1024)]
            corner[s] = others
            if count == 2:
                near[4 + s] = others

    parts = ((4, 16, 1024), F32, VMEM)
    return call(
        f"gathered_z_{c}",
        body,
        [(own, VMEM), (rest, VMEM), (holder[0], SMEM), (holder[1], SMEM), (below, VMEM), (above, VMEM)]
        + [(array, VMEM) for array in after],
        [((16, 8192), F32, VMEM), ((4 * count, 16, 1024), F32, VMEM), parts, parts],
        [pltpu.VMEM((16, 8192), F32)],
    )


def for_holders(holder, mine, beside, corner, near, after=()):
    def body(holder, mine, beside, corner, near, *refs):
        outs = refs[len(after) :]
        for s in range(4):
            outs[s][0] = mine[:, pl.ds(column_of(holder, 0, s), 1024)] + near[s]
            outs[s][1] = beside[s] + corner[s]

    return call(
        "for_holders",
        body,
        [(holder, SMEM)] + [(array, VMEM) for array in (mine, beside, corner, near, *after)],
        [((2, 16, 1024), F32, VMEM)] * 4,
    )


def old_parts(name, holder, states, asked, after):
    def body(holder, weight, first, second, *refs):
        outs = refs[len(after) :]
        for out, steps in zip(outs, asked):
            for i, (a, s) in enumerate(steps):
                start = column_of(holder, a, s)

                def copy(columns):
                    source = pl.ds(pl.multiple_of(start + columns.start, 128), columns.size)
                    for k, old in enumerate((weight, first, second)):
                        out[i, k, :, columns] = old[0, :, source]

                by_tiles(1024, 256, copy)

    return call(
        name,
        body,
        [(holder, SMEM)] + [(old, VMEM) for old in states] + after,
        [((len(steps), 3, 32, 1024), F32, VMEM) for steps in asked],
    )


def old_two(holder, weight, first, second, beside, after):
    def body(holder, weight, first, second, beside, after, out):
        start = column_of(holder, 0, 2)

        def copy(columns):
            source = pl.ds(pl.multiple_of(start + columns.start, 128), columns.size)
            for k, old in enumerate((weight, first, second)):
                out[0, k, :, columns] = old[0, :, source]
                out[1, k, :, columns] = beside[1, k, :, columns]

        by_tiles(1024, 256, copy)

    return call(
        "old_two",
        body,
        [(holder, SMEM)] + [(array, VMEM) for array in (weight, first, second, beside, after)],
        [((2, 3, 32, 1024), F32, VMEM)],
    )[0]


def other_side(olds, after):
    count = len(olds)

    def body(*refs):
        out = refs[count + len(after)]
        for i, old in enumerate(olds):

            def copy(columns):
                for k in range(3):
                    out[i, k, :, columns] = refs[i][old.shape[0] - 1, k, :, columns]

            by_tiles(1024, 256, copy)

    return call(
        "other_side",
        body,
        [(old, VMEM) for old in olds] + after,
        [((count, 3, 32, 1024), F32, VMEM)],
    )[0]


def advance(weight, first, second, grad):
    first_new = 0.9 * first + 0.1 * grad
    second_new = 0.95 * second + 0.05 * (grad * grad)
    root = jnp.sqrt(second_new * (1.0 / (1.0 - 0.95**10))) + 1e-08
    step = (first_new * (0.01 / (1.0 - 0.9**10))) * pl.reciprocal(root, approx=True)
    return (1.0 - 0.01 * 0.1) * weight - step, first_new, second_new


def update(holder, weight, first, second, mine, across, after):
    def body(holder, after, weight, first, second, mine_0, mine_1, all_0, near_1, far_1, *refs):
        outs, made, sems = refs[:3], refs[3], refs[4]
        writes = []
        for c, mine in enumerate((mine_0, mine_1)):
            rows = pl.ds(16 * c, 16)
            for i in range(8):
                columns = pl.ds(column_of(holder, i // 4, i % 4), 1024)
                more = all_0[i] if c == 0 else (near_1, far_1)[i // 4][i % 4]
                new = advance(*(old[0, rows, columns] for old in (weight, first, second)), mine[:, columns] + more)
                for k in range(3):
                    made[k, rows, columns] = new[k]
            for k in range(3):
                copy = pltpu.make_async_copy(made.at[k, rows], outs[k].at[0, rows], sems.at[3 * c + k])
                copy.start()
                writes.append(copy)
        for copy in writes:
            copy.wait()

    return call(
        "update",
        body,
        [(holder, SMEM)] + [(array, VMEM) for array in (after, weight, first, second, *mine, *across)],
        [((1, 32, 8192), F32, HBM)] * 3,
        [pltpu.VMEM((3, 32, 8192), F32), pltpu.SemaphoreType.DMA((6,))],
    )


def encode(code, old, grads, c, into=None):
    arrays, places = [], [[None] * 4, [None] * 4]
    for a in range(2):
        for s in range(4):
            array, part = old[a][s]
            known = [i for i, other in enumerate(arrays) if other is array]
            if not known:
                arrays.append(array)
            places[a][s] = (known[0] if known else len(arrays) - 1, part)

    def body(code, *refs):
        olds, ins, (out, total, sems) = refs[: len(arrays)], refs[len(arrays) :], (refs[-4], *refs[-2:])
        _, _, _, side, y = position()
        ranks = [[lax.rem(side + a, 2) * 4 + lax.rem(y + 4 - s, 4) for s in range(4)] for a in range(2)]
        scales = [[[code[j, ranks[a][s]] for s in range(4)] for a in range(2)] for j in range(4)]

        def state(s, a, k, row, columns):
            array, part = places[a][s]
            return olds[array][part, k, pl.ds(16 * c + row, 8), columns]

        copies = []
        for row in range(0, 16, 8):

            def one(columns):
                rows = pl.ds(row, 8)
                sums = [[None] * 3 for _ in range(4)]
                for s in range(4):
                    for a in range(2):
                        was = [state(s, a, k, row, columns) for k in range(3)]
                        states = advance(*was, ins[s][a, rows, columns])
                        for j in range(4):
                            for k in range(3):
                                term = scales[j][a][s] * states[k]
                                sums[j][k] = term if sums[j][k] is None else sums[j][k] + term
                for j in range(4):
                    for k in range(3):
                        total[j, k, rows, columns] = sums[j][k]

            by_tiles(1024, 256, one)
            there = out.at[:, :, pl.ds(16 * c + row, 8)]
            copies.append(pltpu.make_async_copy(total.at[:, :, pl.ds(row, 8)], there, sems.at[row // 8]))
            copies[-1].start()
        for copy in copies:
            copy.wait()
        refs[-3][...] = jnp.zeros((8, 128), F32)

    return call(
        f"encode_{c}",
        body,
        [(code, SMEM)] + [(array, VMEM) for array in (*arrays, *grads)] + ([] if into is None else [(into, HBM)]),
        [((4, 3, 32, 1024), F32, HBM), ((8, 128), F32, VMEM)],
        [pltpu.VMEM((4, 3, 16, 1024), F32), pltpu.SemaphoreType.DMA((2,))],
        aliases=None if into is None else {1 + len(arrays) + len(grads): 0},
    )


def local(grad_part, weight, moment_one, moment_two, code, owner, holder):
    blocks = grad_part.reshape(16, 32, 8192)
    states = (weight, moment_one, moment_two)

    far, own = widen_far(blocks, owner)
    rest = widen_rest(blocks, owner, far)
    go_up, go_down, rest = pair_far(own, send(far, TO_CORE), rest)
    rest = send(rest, TO_CORE)
    far_below, far_above = send(go_up, UP_Z), send(go_down, DOWN_Z)

    held = send(holder, ACROSS)
    asked = [[(0, 0)], [(1, 0), (1, 2)]]
    zero, beside = old_parts("old_here", holder, states, asked, [(go_up, VMEM), (held, SMEM)])
    (one,) = old_parts("old_one", holder, states, [[(0, 1), (1, 1)]], [(beside, VMEM)])
    (three,) = old_parts("old_three", holder, states, [[(0, 3), (1, 3)]], [(rest, VMEM)])
    own = own_rest(blocks, owner, three)
    beside, one, three = send(beside, BESIDE), send(one, ALONG_Y[1]), send(three, ALONG_Y[3])

    go_up, go_down = onward(own, rest, far_below, far_above, 0, (beside,))
    along_z = [(send(go_up, UP_Z), send(go_down, DOWN_Z))]
    odd = other_side([one, three], [(go_up, VMEM)])
    two = old_two(holder, *states, beside, odd)
    after = (two,)
    odd, two = send(odd, BESIDE), send(two, ALONG_Y[2])
    go_up, go_down = onward(own, rest, far_below, far_above, 1, after)
    along_z.append((send(go_up, UP_Z), send(go_down, DOWN_Z)))
    old = [[(zero, 0), (one, 0), (two, 0), (three, 0)], [(beside, 0), (odd, 0), (two, 1), (odd, 1)]]

    mine, across, parity, after = [], [], None, (two,)
    for c in range(2):
        before = (odd,) if c == 0 else (sums[1],)
        ours, near, to_beside, corner = gathered_z(own, rest, (holder, held), *along_z[c], c, before)
        mine.append(ours)
        to_beside, to_corner, near = send(to_beside, BESIDE), send(corner, CORNER), send(near, ACROSS)
        across.append(near)
        sums = for_holders(holder, ours, to_beside, to_corner, near, after)
        grads = [sums[0]] + [send(sums[s], ALONG_Y[s]) for s in (1, 2, 3)]
        parity, mark = encode(code, old, grads, c, parity)
        after = (mark,)
    across.append(send(corner, ACROSS))

    new = update(holder, *states, mine, across, sums[1])
    return (*new, parity)


def solution(mesh):
    in_specs = (
        P("rack", "dp", None, None),
        P("rack", "dp", None),
        P("rack", "dp", None),
        P("rack", "dp", None),
        P(),
        P("rack", None),
        P("dp", None),
    )
    out_specs = (
        P("rack", "dp", None),
        P("rack", "dp", None),
        P("rack", "dp", None),
        P(None, None, "dp", "rack"),
    )
    return jax.shard_map(local, mesh=mesh, in_specs=in_specs, out_specs=out_specs, check_vma=False)
```

```python
import jax
import jax.numpy as jnp
from jax import lax
from jax.experimental import pallas as pl
from jax.experimental.pallas import tpu as pltpu
from jax.sharding import PartitionSpec as P

AXES = ("rack", "dp")
F32, BF16 = jnp.float32, jnp.bfloat16
MIB = 1 << 20
VMEM = pl.BlockSpec(memory_space=pltpu.VMEM)
SMEM = pl.BlockSpec(memory_space=pltpu.SMEM)
HBM = pl.BlockSpec(memory_space=pltpu.HBM)


def links(move):
    pairs = []
    for rack in range(8):
        for data in range(16):
            x, y, z, core = (data // 2 % 2) * 2 + rack // 4, rack % 4, data // 4, data % 2
            nx, ny, nz, ncore = move(x, y, z, core)
            nx, ny, nz = nx % 4, ny % 4, nz % 4
            pairs.append((rack * 16 + data, ((nx % 2) * 4 + ny) * 16 + nz * 4 + (nx // 2) * 2 + ncore))
    return pairs


TO_CORE = links(lambda x, y, z, core: (x, y, z, 1 - core))
UP_Z = links(lambda x, y, z, core: (x, y, z + 1, core))
DOWN_Z = links(lambda x, y, z, core: (x, y, z - 1, core))
ACROSS = links(lambda x, y, z, core: (x ^ 2, y, z, core))
BESIDE = links(lambda x, y, z, core: (x ^ 1, y, z, core))
CORNER = links(lambda x, y, z, core: (3 - x, y, z, core))
ALONG_Y = [None] + [links(lambda x, y, z, core, step=step: (x, y + step, z, core)) for step in (1, 2, 3)]

RELATIVE_Z = (2, 1, 3, 0)
FAR, UP, DOWN, HERE = 0, 2, 4, 6


def send(array, pairs):
    return lax.ppermute(array, AXES, pairs)


def call(name, body, ins, outs, scratch=(), aliases=None, limit=16):
    return pl.pallas_call(
        body,
        out_shape=[jax.ShapeDtypeStruct(shape, kind) for shape, kind, _ in outs],
        in_specs=[spec for _, spec in ins],
        out_specs=[spec for _, _, spec in outs],
        scratch_shapes=list(scratch),
        input_output_aliases=aliases or {},
        compiler_params=pltpu.CompilerParams(vmem_limit_bytes=limit * MIB),
        name=name,
    )(*[array for array, _ in ins])


def position():
    data, rack = lax.axis_index("dp"), lax.axis_index("rack")
    return lax.div(data, 4), lax.rem(lax.div(data, 2), 2), lax.rem(data, 2), lax.div(rack, 4), lax.rem(rack, 4)


def found(row, count, value):
    at = jnp.int32(0)
    for i in range(count):
        at = jnp.where(row[0, i] == value, i, at)
    return at


def block_of(owner, slot, keep):
    z, half, core, _, _ = position()
    whose = core if keep else 1 - core
    target = lax.rem(z + RELATIVE_Z[slot // 2], 4) * 4 + lax.rem(half + slot % 2, 2) * 2 + whose
    return found(owner, 16, target)


def column_of(holder, side_step, y_step):
    _, _, _, side, y = position()
    rank = lax.rem(side + side_step, 2) * 4 + lax.rem(y + y_step, 4)
    return pl.multiple_of(found(holder, 8, rank) * 1024, 1024)


def by_tiles(width, step, body):
    def one(i, carry):
        body(pl.ds(pl.multiple_of(i * step, step), step))
        return carry

    lax.fori_loop(0, width // step, one, 0)


def widen_far(blocks, owner):
    def body(blocks, owner, out, read, sems):
        copies = [
            pltpu.make_async_copy(blocks.at[block_of(owner, FAR + i, False)], read.at[i], sems.at[i]) for i in range(2)
        ]
        for copy in copies:
            copy.start()
        for i in range(2):
            copies[i].wait()

            def cast(columns):
                out[i, :, columns] = read[i, :, columns].astype(F32)

            by_tiles(8192, 1024, cast)

    return call(
        "widen_far",
        body,
        [(blocks, HBM), (owner, SMEM)],
        [((2, 32, 8192), F32, VMEM)],
        [pltpu.VMEM((2, 32, 8192), BF16), pltpu.SemaphoreType.DMA((2,))],
        limit=50,
    )[0]


def widen_rest(blocks, owner, far):
    def body(blocks, owner, far, out, own, read, sems):
        copies = [
            pltpu.make_async_copy(blocks.at[block_of(owner, UP + i, False)], read.at[i], sems.at[i]) for i in range(6)
        ] + [pltpu.make_async_copy(blocks.at[block_of(owner, i, True)], own.at[i], sems.at[6 + i]) for i in range(8)]
        for copy in copies:
            copy.start()
        for i in range(6):
            copies[i].wait()

            def cast(columns):
                out[i, :, columns] = read[i, :, columns].astype(F32)

            by_tiles(8192, 1024, cast)
        for copy in copies[6:]:
            copy.wait()

    return call(
        "widen_rest",
        body,
        [(blocks, HBM), (owner, SMEM), (far, VMEM)],
        [((6, 32, 8192), F32, VMEM), ((8, 32, 8192), BF16, VMEM)],
        [pltpu.VMEM((6, 32, 8192), BF16), pltpu.SemaphoreType.DMA((14,))],
        limit=40,
    )


def pair_far(own, far, rest):
    def body(own, far, rest, up, down, same):
        for j in range(2):

            def add(columns):
                later = pl.ds(columns.start + 4096, columns.size)
                up[j, :, columns] = own[FAR + j, :, columns].astype(F32) + far[j, :, columns]
                down[j, :, columns] = own[FAR + j, :, later].astype(F32) + far[j, :, later]

            by_tiles(4096, 512, add)

    half = ((2, 32, 4096), F32, VMEM)
    return call(
        "pair_far",
        body,
        [(own, VMEM), (far, VMEM), (rest, VMEM)],
        [half, half, (rest.shape, F32, VMEM)],
        aliases={2: 2},
    )


def onward(own, rest, below, above, c, after=()):
    def body(own, rest, below, above, *refs):
        up, down = refs[len(after) :]
        rows = pl.ds(16 * c, 16)

        def pair(slot, columns):
            return own[slot, rows, columns].astype(F32) + rest[slot - 2, rows, columns]

        for j in range(2):

            def add(columns):
                later = pl.ds(columns.start + 4096, columns.size)
                up[0, j, :, columns] = pair(UP + j, columns) + below[j, rows, columns]
                up[1, j, :, columns] = pair(UP + j, later)
                down[0, j, :, columns] = pair(DOWN + j, later) + above[j, rows, columns]
                down[1, j, :, columns] = pair(DOWN + j, columns)

            by_tiles(4096, 512, add)

    half = ((2, 2, 16, 4096), F32, VMEM)
    return call(
        f"onward_{c}",
        body,
        [(own, VMEM), (rest, VMEM), (below, VMEM), (above, VMEM)] + [(array, VMEM) for array in after],
        [half, half],
    )


def gathered_z(own, rest, holder, below, above, c, after):
    count = 2 - c

    def body(own, rest, mine_held, other_held, below, above, *refs):
        mine, near, beside, corner, theirs = refs[len(after) :]
        rows = pl.ds(16 * c, 16)
        for j, out in enumerate((mine, theirs)):

            def add(columns):
                later = pl.ds(columns.start + 4096, columns.size)
                both = own[HERE + j, rows, columns].astype(F32) + rest[HERE - 2 + j, rows, columns]
                out[:, columns] = both + below[0, j, :, columns] + above[1, j, :, columns]
                both = own[HERE + j, rows, later].astype(F32) + rest[HERE - 2 + j, rows, later]
                out[:, later] = both + below[1, j, :, columns] + above[0, j, :, columns]

            by_tiles(4096, 512, add)
        for s in range(4):
            beside[s] = mine[:, pl.ds(column_of(mine_held, 1, s), 1024)]
            near[s] = theirs[:, pl.ds(column_of(other_held, 0, s), 1024)]
            others = theirs[:, pl.ds(column_of(other_held, 1, s), 1024)]
            corner[s] = others
            if count == 2:
                near[4 + s] = others

    parts = ((4, 16, 1024), F32, VMEM)
    return call(
        f"gathered_z_{c}",
        body,
        [(own, VMEM), (rest, VMEM), (holder[0], SMEM), (holder[1], SMEM), (below, VMEM), (above, VMEM)]
        + [(array, VMEM) for array in after],
        [((16, 8192), F32, VMEM), ((4 * count, 16, 1024), F32, VMEM), parts, parts],
        [pltpu.VMEM((16, 8192), F32)],
    )


def for_holders(holder, mine, near, beside, corner, after):
    def body(holder, mine, near, beside, corner, after, *outs):
        for s in range(4):
            outs[s][0] = mine[:, pl.ds(column_of(holder, 0, s), 1024)] + near[s]
            outs[s][1] = beside[s] + corner[s]

    return call(
        "for_holders",
        body,
        [(holder, SMEM)] + [(array, VMEM) for array in (mine, near, beside, corner, after)],
        [((2, 16, 1024), F32, VMEM)] * 4,
    )


def old_parts(name, holder, states, asked, after):
    def body(holder, weight, first, second, *refs):
        outs = refs[len(after) :]
        for out, steps in zip(outs, asked):
            for i, (a, s) in enumerate(steps):
                start = column_of(holder, a, s)

                def copy(columns):
                    source = pl.ds(pl.multiple_of(start + columns.start, 128), columns.size)
                    for k, old in enumerate((weight, first, second)):
                        out[i, k, :, columns] = old[0, :, source]

                by_tiles(1024, 256, copy)

    return call(
        name,
        body,
        [(holder, SMEM)] + [(old, VMEM) for old in states] + [(array, VMEM) for array in after],
        [((len(steps), 3, 32, 1024), F32, VMEM) for steps in asked],
    )


def other_side(olds, after):
    count = len(olds)

    def body(*refs):
        out = refs[count + len(after)]
        for i in range(count):

            def copy(columns):
                for k in range(3):
                    out[i, k, :, columns] = refs[i][1, k, :, columns]

            by_tiles(1024, 256, copy)

    return call(
        "other_side",
        body,
        [(old, VMEM) for old in olds] + after,
        [((count, 3, 32, 1024), F32, VMEM)],
    )[0]


def advance(weight, first, second, grad):
    first_new = 0.9 * first + 0.1 * grad
    second_new = 0.95 * second + 0.05 * (grad * grad)
    root = jnp.sqrt(second_new * (1.0 / (1.0 - 0.95**10))) + 1e-08
    step = (first_new * (0.01 / (1.0 - 0.9**10))) * pl.reciprocal(root, approx=True)
    return (1.0 - 0.01 * 0.1) * weight - step, first_new, second_new


def update(holder, weight, first, second, mine, across):
    def body(holder, weight, first, second, mine_0, mine_1, all_0, near_1, far_1, *refs):
        outs, made, sems = refs[:3], refs[3], refs[4]
        writes = []
        for c, mine in enumerate((mine_0, mine_1)):
            rows = pl.ds(16 * c, 16)
            for i in range(8):
                columns = pl.ds(column_of(holder, i // 4, i % 4), 1024)
                more = all_0[i] if c == 0 else (near_1, far_1)[i // 4][i % 4]
                new = advance(*(old[0, rows, columns] for old in (weight, first, second)), mine[:, columns] + more)
                for k in range(3):
                    made[k, rows, columns] = new[k]
            for k in range(3):
                copy = pltpu.make_async_copy(made.at[k, rows], outs[k].at[0, rows], sems.at[3 * c + k])
                copy.start()
                writes.append(copy)
        for copy in writes:
            copy.wait()

    return call(
        "update",
        body,
        [(holder, SMEM)] + [(array, VMEM) for array in (weight, first, second, *mine, *across)],
        [((1, 32, 8192), F32, HBM)] * 3,
        [pltpu.VMEM((3, 32, 8192), F32), pltpu.SemaphoreType.DMA((6,))],
    )


def encode(code, old, grads, c, into=None):
    arrays, places = [], [[None] * 4, [None] * 4]
    for a in range(2):
        for s in range(4):
            array, part = old[a][s]
            known = [i for i, other in enumerate(arrays) if other is array]
            if not known:
                arrays.append(array)
            places[a][s] = (known[0] if known else len(arrays) - 1, part)

    def body(code, *refs):
        olds, ins, (out, total, sems) = refs[: len(arrays)], refs[len(arrays) :], (refs[-4], *refs[-2:])
        _, _, _, side, y = position()
        ranks = [[lax.rem(side + a, 2) * 4 + lax.rem(y + 4 - s, 4) for s in range(4)] for a in range(2)]
        scales = [[[code[j, ranks[a][s]] for s in range(4)] for a in range(2)] for j in range(4)]

        def state(s, a, k, row, columns):
            array, part = places[a][s]
            return olds[array][part, k, pl.ds(16 * c + row, 8), columns]

        copies = []
        for row in range(0, 16, 8):

            def one(columns):
                rows = pl.ds(row, 8)
                sums = [[None] * 3 for _ in range(4)]
                for s in range(4):
                    for a in range(2):
                        was = [state(s, a, k, row, columns) for k in range(3)]
                        states = advance(*was, ins[s][a, rows, columns])
                        for j in range(4):
                            for k in range(3):
                                term = scales[j][a][s] * states[k]
                                sums[j][k] = term if sums[j][k] is None else sums[j][k] + term
                for j in range(4):
                    for k in range(3):
                        total[j, k, rows, columns] = sums[j][k]

            for lane in range(0, 1024, 256):
                one(pl.ds(lane, 256))
                there = out.at[:, :, pl.ds(16 * c + row, 8), pl.ds(lane, 256)]
                made = total.at[:, :, pl.ds(row, 8), pl.ds(lane, 256)]
                copies.append(pltpu.make_async_copy(made, there, sems.at[len(copies)]))
                copies[-1].start()
        for copy in copies:
            copy.wait()
        refs[-3][...] = jnp.zeros((8, 128), F32)

    return call(
        f"encode_{c}",
        body,
        [(code, SMEM)] + [(array, VMEM) for array in (*arrays, *grads)] + ([] if into is None else [(into, HBM)]),
        [((4, 3, 32, 1024), F32, HBM), ((8, 128), F32, VMEM)],
        [pltpu.VMEM((4, 3, 16, 1024), F32), pltpu.SemaphoreType.DMA((8,))],
        aliases=None if into is None else {1 + len(arrays) + len(grads): 0},
    )


def local(grad_part, weight, moment_one, moment_two, code, owner, holder):
    blocks = grad_part.reshape(16, 32, 8192)
    states = (weight, moment_one, moment_two)

    far = widen_far(blocks, owner)
    rest, own = widen_rest(blocks, owner, far)
    go_up, go_down, rest = pair_far(own, send(far, TO_CORE), rest)
    rest = send(rest, TO_CORE)
    far_below, far_above = send(go_up, UP_Z), send(go_down, DOWN_Z)

    one, three = old_parts("old_odd", holder, states, [[(0, 1), (1, 1)], [(0, 3), (1, 3)]], (go_up,))
    one, three = send(one, ALONG_Y[1]), send(three, ALONG_Y[3])
    zero, beside = old_parts("old_here", holder, states, [[(0, 0)], [(1, 0)]], (rest,))
    beside = send(beside, BESIDE)

    held = send(holder, ACROSS)
    odd = other_side([one, three], [(beside, VMEM)])
    (two,) = old_parts("old_two", holder, states, [[(0, 2), (1, 2)]], (odd,))
    after = (two,)
    odd, two = send(odd, BESIDE), send(two, ALONG_Y[2])

    go_up, go_down = onward(own, rest, far_below, far_above, 0, after)
    along_z = [(send(go_up, UP_Z), send(go_down, DOWN_Z))]
    even = other_side([two], [(odd, VMEM), (go_up, VMEM), (held, SMEM)])
    after = (even,)
    even = send(even, BESIDE)
    go_up, go_down = onward(own, rest, far_below, far_above, 1, after)
    along_z.append((send(go_up, UP_Z), send(go_down, DOWN_Z)))
    old = [[(zero, 0), (one, 0), (two, 0), (three, 0)], [(beside, 0), (odd, 0), (even, 0), (odd, 1)]]

    mine, across, parity = [], [], None
    for c in range(2):
        ours, near, to_beside, to_corner = gathered_z(own, rest, (holder, held), *along_z[c], c, after)
        mine.append(ours)
        across.append(send(near, ACROSS))
        done = even if c == 0 else done
        sums = for_holders(holder, ours, across[c], send(to_beside, BESIDE), send(to_corner, CORNER), done)
        after = (sums[1],)
        grads = [sums[0]] + [send(sums[s], ALONG_Y[s]) for s in (1, 2, 3)]
        parity, done = encode(code, old, grads, c, parity)
    across.append(send(to_corner, ACROSS))

    new = update(holder, *states, mine, across)
    return (*new, parity)


def solution(mesh):
    in_specs = (
        P("rack", "dp", None, None),
        P("rack", "dp", None),
        P("rack", "dp", None),
        P("rack", "dp", None),
        P(),
        P("rack", None),
        P("dp", None),
    )
    out_specs = (
        P("rack", "dp", None),
        P("rack", "dp", None),
        P("rack", "dp", None),
        P(None, None, "dp", "rack"),
    )
    return jax.shard_map(local, mesh=mesh, in_specs=in_specs, out_specs=out_specs, check_vma=False)
```

```python
import jax
import jax.numpy as jnp
from jax import lax
from jax.experimental import pallas as pl
from jax.experimental.pallas import tpu as pltpu
from jax.sharding import PartitionSpec as P

AXES = ("rack", "dp")
F32, BF16 = jnp.float32, jnp.bfloat16
MIB = 1 << 20
VMEM = pl.BlockSpec(memory_space=pltpu.VMEM)
SMEM = pl.BlockSpec(memory_space=pltpu.SMEM)
HBM = pl.BlockSpec(memory_space=pltpu.HBM)


def links(move):
    pairs = []
    for rack in range(8):
        for data in range(16):
            x, y, z, core = (data // 2 % 2) * 2 + rack // 4, rack % 4, data // 4, data % 2
            nx, ny, nz, ncore = move(x, y, z, core)
            nx, ny, nz = nx % 4, ny % 4, nz % 4
            pairs.append((rack * 16 + data, ((nx % 2) * 4 + ny) * 16 + nz * 4 + (nx // 2) * 2 + ncore))
    return pairs


TO_CORE = links(lambda x, y, z, core: (x, y, z, 1 - core))
UP_Z = links(lambda x, y, z, core: (x, y, z + 1, core))
DOWN_Z = links(lambda x, y, z, core: (x, y, z - 1, core))
ACROSS = links(lambda x, y, z, core: (x ^ 2, y, z, core))
BESIDE = links(lambda x, y, z, core: (x ^ 1, y, z, core))
CORNER = links(lambda x, y, z, core: (3 - x, y, z, core))
ALONG_Y = [None] + [links(lambda x, y, z, core, step=step: (x, y + step, z, core)) for step in (1, 2, 3)]

RELATIVE_Z = (2, 1, 3, 0)
FAR, UP, DOWN, HERE = 0, 2, 4, 6


def send(array, pairs):
    return lax.ppermute(array, AXES, pairs)


def call(name, body, ins, outs, scratch=(), aliases=None, limit=16):
    return pl.pallas_call(
        body,
        out_shape=[jax.ShapeDtypeStruct(shape, kind) for shape, kind, _ in outs],
        in_specs=[spec for _, spec in ins],
        out_specs=[spec for _, _, spec in outs],
        scratch_shapes=list(scratch),
        input_output_aliases=aliases or {},
        compiler_params=pltpu.CompilerParams(vmem_limit_bytes=limit * MIB),
        name=name,
    )(*[array for array, _ in ins])


def position():
    data, rack = lax.axis_index("dp"), lax.axis_index("rack")
    return lax.div(data, 4), lax.rem(lax.div(data, 2), 2), lax.rem(data, 2), lax.div(rack, 4), lax.rem(rack, 4)


def found(row, count, value):
    at = jnp.int32(0)
    for i in range(count):
        at = jnp.where(row[0, i] == value, i, at)
    return at


def block_of(owner, slot, keep):
    z, half, core, _, _ = position()
    whose = core if keep else 1 - core
    target = lax.rem(z + RELATIVE_Z[slot // 2], 4) * 4 + lax.rem(half + slot % 2, 2) * 2 + whose
    return found(owner, 16, target)


def column_of(holder, side_step, y_step):
    _, _, _, side, y = position()
    rank = lax.rem(side + side_step, 2) * 4 + lax.rem(y + y_step, 4)
    return pl.multiple_of(found(holder, 8, rank) * 1024, 1024)


def by_tiles(width, step, body):
    def one(i, carry):
        body(pl.ds(pl.multiple_of(i * step, step), step))
        return carry

    lax.fori_loop(0, width // step, one, 0)


def widen_far(blocks, owner):
    def body(blocks, owner, out, read, sems):
        copies = [
            pltpu.make_async_copy(blocks.at[block_of(owner, FAR + i, False)], read.at[i], sems.at[i]) for i in range(2)
        ]
        for copy in copies:
            copy.start()
        for i in range(2):
            copies[i].wait()

            def cast(columns):
                out[i, :, columns] = read[i, :, columns].astype(F32)

            by_tiles(8192, 1024, cast)

    return call(
        "widen_far",
        body,
        [(blocks, HBM), (owner, SMEM)],
        [((2, 32, 8192), F32, VMEM)],
        [pltpu.VMEM((2, 32, 8192), BF16), pltpu.SemaphoreType.DMA((2,))],
        limit=50,
    )[0]


def widen_rest(blocks, owner, far):
    def body(blocks, owner, far, out, own, read, sems):
        copies = [
            pltpu.make_async_copy(blocks.at[block_of(owner, UP + i, False)], read.at[i], sems.at[i]) for i in range(6)
        ] + [pltpu.make_async_copy(blocks.at[block_of(owner, i, True)], own.at[i], sems.at[6 + i]) for i in range(8)]
        for copy in copies:
            copy.start()
        for i in range(6):
            copies[i].wait()

            def cast(columns):
                out[i, :, columns] = read[i, :, columns].astype(F32)

            by_tiles(8192, 1024, cast)
        for copy in copies[6:]:
            copy.wait()

    return call(
        "widen_rest",
        body,
        [(blocks, HBM), (owner, SMEM), (far, VMEM)],
        [((6, 32, 8192), F32, VMEM), ((8, 32, 8192), BF16, VMEM)],
        [pltpu.VMEM((6, 32, 8192), BF16), pltpu.SemaphoreType.DMA((14,))],
        limit=40,
    )


def pair_far(own, far, rest):
    def body(own, far, rest, up, down, same):
        for j in range(2):

            def add(columns):
                later = pl.ds(columns.start + 4096, columns.size)
                up[j, :, columns] = own[FAR + j, :, columns].astype(F32) + far[j, :, columns]
                down[j, :, columns] = own[FAR + j, :, later].astype(F32) + far[j, :, later]

            by_tiles(4096, 512, add)

    half = ((2, 32, 4096), F32, VMEM)
    return call(
        "pair_far",
        body,
        [(own, VMEM), (far, VMEM), (rest, VMEM)],
        [half, half, (rest.shape, F32, VMEM)],
        aliases={2: 2},
    )


def onward(own, rest, below, above, c, after=()):
    def body(own, rest, below, above, *refs):
        up, down = refs[len(after) :]
        rows = pl.ds(16 * c, 16)

        def pair(slot, columns):
            return own[slot, rows, columns].astype(F32) + rest[slot - 2, rows, columns]

        for j in range(2):

            def add(columns):
                later = pl.ds(columns.start + 4096, columns.size)
                up[0, j, :, columns] = pair(UP + j, columns) + below[j, rows, columns]
                up[1, j, :, columns] = pair(UP + j, later)
                down[0, j, :, columns] = pair(DOWN + j, later) + above[j, rows, columns]
                down[1, j, :, columns] = pair(DOWN + j, columns)

            by_tiles(4096, 512, add)

    half = ((2, 2, 16, 4096), F32, VMEM)
    return call(
        f"onward_{c}",
        body,
        [(own, VMEM), (rest, VMEM), (below, VMEM), (above, VMEM)] + [(array, VMEM) for array in after],
        [half, half],
    )


def gathered_z(own, rest, holder, below, above, c, after):
    count = 2 - c

    def body(own, rest, mine_held, other_held, below, above, *refs):
        mine, near, beside, corner, theirs = refs[len(after) :]
        rows = pl.ds(16 * c, 16)
        for j, out in enumerate((mine, theirs)):

            def add(columns):
                later = pl.ds(columns.start + 4096, columns.size)
                both = own[HERE + j, rows, columns].astype(F32) + rest[HERE - 2 + j, rows, columns]
                out[:, columns] = both + below[0, j, :, columns] + above[1, j, :, columns]
                both = own[HERE + j, rows, later].astype(F32) + rest[HERE - 2 + j, rows, later]
                out[:, later] = both + below[1, j, :, columns] + above[0, j, :, columns]

            by_tiles(4096, 512, add)
        for s in range(4):
            beside[s] = mine[:, pl.ds(column_of(mine_held, 1, s), 1024)]
            near[s] = theirs[:, pl.ds(column_of(other_held, 0, s), 1024)]
            others = theirs[:, pl.ds(column_of(other_held, 1, s), 1024)]
            corner[s] = others
            if count == 2:
                near[4 + s] = others

    parts = ((4, 16, 1024), F32, VMEM)
    return call(
        f"gathered_z_{c}",
        body,
        [(own, VMEM), (rest, VMEM), (holder[0], SMEM), (holder[1], SMEM), (below, VMEM), (above, VMEM)]
        + [(array, VMEM) for array in after],
        [((16, 8192), F32, VMEM), ((4 * count, 16, 1024), F32, VMEM), parts, parts],
        [pltpu.VMEM((16, 8192), F32)],
    )


def for_holders(holder, mine, near, beside, corner, after):
    def body(holder, mine, near, beside, corner, after, *outs):
        for s in range(4):
            outs[s][0] = mine[:, pl.ds(column_of(holder, 0, s), 1024)] + near[s]
            outs[s][1] = beside[s] + corner[s]

    return call(
        "for_holders",
        body,
        [(holder, SMEM)] + [(array, VMEM) for array in (mine, near, beside, corner, after)],
        [((2, 16, 1024), F32, VMEM)] * 4,
    )


def old_parts(name, holder, states, asked, after):
    def body(holder, weight, first, second, *refs):
        outs = refs[len(after) :]
        for out, steps in zip(outs, asked):
            for i, (a, s) in enumerate(steps):
                start = column_of(holder, a, s)

                def copy(columns):
                    source = pl.ds(pl.multiple_of(start + columns.start, 128), columns.size)
                    for k, old in enumerate((weight, first, second)):
                        out[i, k, :, columns] = old[0, :, source]

                by_tiles(1024, 256, copy)

    return call(
        name,
        body,
        [(holder, SMEM)] + [(old, VMEM) for old in states] + [(array, VMEM) for array in after],
        [((len(steps), 3, 32, 1024), F32, VMEM) for steps in asked],
    )


def other_side(olds, after):
    count = len(olds)

    def body(*refs):
        out = refs[count + len(after)]
        for i in range(count):

            def copy(columns):
                for k in range(3):
                    out[i, k, :, columns] = refs[i][1, k, :, columns]

            by_tiles(1024, 256, copy)

    return call(
        "other_side",
        body,
        [(old, VMEM) for old in olds] + after,
        [((count, 3, 32, 1024), F32, VMEM)],
    )[0]


def advance(weight, first, second, grad):
    first_new = 0.9 * first + 0.1 * grad
    second_new = 0.95 * second + 0.05 * (grad * grad)
    root = jnp.sqrt(second_new * (1.0 / (1.0 - 0.95**10))) + 1e-08
    step = (first_new * (0.01 / (1.0 - 0.9**10))) * pl.reciprocal(root, approx=True)
    return (1.0 - 0.01 * 0.1) * weight - step, first_new, second_new


def update(holder, weight, first, second, mine, across):
    def body(holder, weight, first, second, mine_0, mine_1, all_0, near_1, far_1, *refs):
        outs, made, sems = refs[:3], refs[3], refs[4]
        writes = []
        for c, mine in enumerate((mine_0, mine_1)):
            rows = pl.ds(16 * c, 16)
            for i in range(8):
                columns = pl.ds(column_of(holder, i // 4, i % 4), 1024)
                more = all_0[i] if c == 0 else (near_1, far_1)[i // 4][i % 4]
                new = advance(*(old[0, rows, columns] for old in (weight, first, second)), mine[:, columns] + more)
                for k in range(3):
                    made[k, rows, columns] = new[k]
            for k in range(3):
                copy = pltpu.make_async_copy(made.at[k, rows], outs[k].at[0, rows], sems.at[3 * c + k])
                copy.start()
                writes.append(copy)
        for copy in writes:
            copy.wait()

    return call(
        "update",
        body,
        [(holder, SMEM)] + [(array, VMEM) for array in (weight, first, second, *mine, *across)],
        [((1, 32, 8192), F32, HBM)] * 3,
        [pltpu.VMEM((3, 32, 8192), F32), pltpu.SemaphoreType.DMA((6,))],
    )


def encode_here(code, old, grad, c):
    def body(code, old_0, old_1, grad, total):
        _, _, _, side, y = position()
        scales = [[code[j, lax.rem(side + a, 2) * 4 + y] for a in range(2)] for j in range(4)]
        for row in range(0, 16, 8):

            def one(columns):
                rows = pl.ds(row, 8)
                states = []
                for a, source in enumerate((old_0, old_1)):
                    was = [source[old[a][1], k, pl.ds(16 * c + row, 8), columns] for k in range(3)]
                    states.append(advance(*was, grad[a, rows, columns]))
                for j in range(4):
                    for k in range(3):
                        total[j, k, rows, columns] = scales[j][0] * states[0][k] + scales[j][1] * states[1][k]

            by_tiles(1024, 256, one)

    return call(
        "encode_here",
        body,
        [(code, SMEM), (old[0][0], VMEM), (old[1][0], VMEM), (grad, VMEM)],
        [((4, 3, 16, 1024), F32, VMEM)],
    )[0]


def encode(code, old, grads, c, into=None, begun=None):
    given = [*grads] if begun is None else [*grads, begun]
    arrays, places = [], [[None] * 4, [None] * 4]
    for a in range(2):
        for s in range(4):
            array, part = old[a][s]
            known = [i for i, other in enumerate(arrays) if other is array]
            if not known:
                arrays.append(array)
            places[a][s] = (known[0] if known else len(arrays) - 1, part)

    def body(code, *refs):
        olds, ins, (out, total, sems) = refs[: len(arrays)], refs[len(arrays) :], (refs[-4], *refs[-2:])
        _, _, _, side, y = position()
        ranks = [[lax.rem(side + a, 2) * 4 + lax.rem(y + 4 - s, 4) for s in range(4)] for a in range(2)]
        scales = [[[code[j, ranks[a][s]] for s in range(4)] for a in range(2)] for j in range(4)]

        def state(s, a, k, row, columns):
            array, part = places[a][s]
            return olds[array][part, k, pl.ds(16 * c + row, 8), columns]

        copies = []
        for row in range(0, 16, 8):

            def one(columns):
                rows = pl.ds(row, 8)
                sums = [[None] * 3 for _ in range(4)]
                if begun is not None:
                    sums = [[ins[4][j, k, rows, columns] for k in range(3)] for j in range(4)]
                for s in range(0 if begun is None else 1, 4):
                    for a in range(2):
                        was = [state(s, a, k, row, columns) for k in range(3)]
                        states = advance(*was, ins[s][a, rows, columns])
                        for j in range(4):
                            for k in range(3):
                                term = scales[j][a][s] * states[k]
                                sums[j][k] = term if sums[j][k] is None else sums[j][k] + term
                for j in range(4):
                    for k in range(3):
                        total[j, k, rows, columns] = sums[j][k]

            for lane in range(0, 1024, 256):
                one(pl.ds(lane, 256))
                there = out.at[:, :, pl.ds(16 * c + row, 8), pl.ds(lane, 256)]
                made = total.at[:, :, pl.ds(row, 8), pl.ds(lane, 256)]
                copies.append(pltpu.make_async_copy(made, there, sems.at[len(copies)]))
                copies[-1].start()
        for copy in copies:
            copy.wait()
        refs[-3][...] = jnp.zeros((8, 128), F32)

    return call(
        f"encode_{c}",
        body,
        [(code, SMEM)] + [(array, VMEM) for array in (*arrays, *given)] + ([] if into is None else [(into, HBM)]),
        [((4, 3, 32, 1024), F32, HBM), ((8, 128), F32, VMEM)],
        [pltpu.VMEM((4, 3, 16, 1024), F32), pltpu.SemaphoreType.DMA((8,))],
        aliases=None if into is None else {1 + len(arrays) + len(given): 0},
    )


def local(grad_part, weight, moment_one, moment_two, code, owner, holder):
    blocks = grad_part.reshape(16, 32, 8192)
    states = (weight, moment_one, moment_two)

    far = widen_far(blocks, owner)
    rest, own = widen_rest(blocks, owner, far)
    go_up, go_down, rest = pair_far(own, send(far, TO_CORE), rest)
    rest = send(rest, TO_CORE)
    far_below, far_above = send(go_up, UP_Z), send(go_down, DOWN_Z)

    one, three = old_parts("old_odd", holder, states, [[(0, 1), (1, 1)], [(0, 3), (1, 3)]], (go_up,))
    one, three = send(one, ALONG_Y[1]), send(three, ALONG_Y[3])
    zero, beside = old_parts("old_here", holder, states, [[(0, 0)], [(1, 0)]], (rest,))
    beside = send(beside, BESIDE)

    held = send(holder, ACROSS)
    odd = other_side([one, three], [(beside, VMEM)])
    (two,) = old_parts("old_two", holder, states, [[(0, 2), (1, 2)]], (odd,))
    after = (two,)
    odd, two = send(odd, BESIDE), send(two, ALONG_Y[2])

    go_up, go_down = onward(own, rest, far_below, far_above, 0, after)
    along_z = [(send(go_up, UP_Z), send(go_down, DOWN_Z))]
    even = other_side([two], [(odd, VMEM), (go_up, VMEM), (held, SMEM)])
    after = (even,)
    even = send(even, BESIDE)
    go_up, go_down = onward(own, rest, far_below, far_above, 1, after)
    along_z.append((send(go_up, UP_Z), send(go_down, DOWN_Z)))
    old = [[(zero, 0), (one, 0), (two, 0), (three, 0)], [(beside, 0), (odd, 0), (even, 0), (odd, 1)]]

    mine, across, parity = [], [], None
    for c in range(2):
        ours, near, to_beside, to_corner = gathered_z(own, rest, (holder, held), *along_z[c], c, after)
        mine.append(ours)
        across.append(send(near, ACROSS))
        done = even if c == 0 else done
        sums = for_holders(holder, ours, across[c], send(to_beside, BESIDE), send(to_corner, CORNER), done)
        after = (sums[1],)
        grads = [sums[0]] + [send(sums[s], ALONG_Y[s]) for s in (1, 2, 3)]
        begun = encode_here(code, [old[0][0], old[1][0]], sums[0], c) if c else None
        parity, done = encode(code, old, grads, c, parity, begun)
    across.append(send(to_corner, ACROSS))

    new = update(holder, *states, mine, across)
    return (*new, parity)


def solution(mesh):
    in_specs = (
        P("rack", "dp", None, None),
        P("rack", "dp", None),
        P("rack", "dp", None),
        P("rack", "dp", None),
        P(),
        P("rack", None),
        P("dp", None),
    )
    out_specs = (
        P("rack", "dp", None),
        P("rack", "dp", None),
        P("rack", "dp", None),
        P(None, None, "dp", "rack"),
    )
    return jax.shard_map(local, mesh=mesh, in_specs=in_specs, out_specs=out_specs, check_vma=False)
```
